32 devices in a mesh: samp: 4 (over y, core), par: 8 (over z, x).
Axes of the slice: x: 2, y: 2, z: 4, core: 2. Of those that a mesh axis runs over, the one named last changes fastest.
Arguments:
- jacobian: bfloat16 [4096, 65536], P(('samp', 'par')), as said below
- sample_slot: int32 [4096], P(('samp', 'par')), may hold values from 0 to 1023, as said below
- panel_index: int32 [1], replicated, may hold values from 0 to 4095
- shift_value: float32 [1], replicated, may hold values from 0.1 to 1
Outputs:
- cholesky_panel: float32 [4096, 1024], P(('samp', 'par'))
The draws below stay inside these ranges and needn't reach their ends.
Inputs may be any that keep to these rules, and one draw needn't show every extreme that they name: Within each group (samples g * 1024 to (g + 1) * 1024 - 1), sample_slot is a permutation of 0 to 1023. `jacobian`: finite values.
All inputs are finite; a program needn't handle non-finite values.
Results may differ from the reference program's by a relative error of at most 0.0003.
Values may be sent and summed in bfloat16 or wider, within the bound.
No kernel may reach another device: no remote copies, remote signals or barrier semaphores. Data moves between devices by JAX's collectives and lax.ppermute only.
A program may use at most 128 MiB of HBM per device.

```python
import math
import jax
import jax.numpy as jnp
from jax import lax

PARAMS = 65536
GROUP = 1024
GROUPS = 4
SAMPLES = 4096


def draw_jacobian(key, part):
    shared_count = 16
    first, second, third = jax.random.split(jax.random.fold_in(key, 11), 3)
    noise = jax.random.normal(first, (SAMPLES, PARAMS), jnp.float32)
    coefs = jax.random.normal(second, (SAMPLES, shared_count), jnp.float32)
    directions = jax.random.normal(third, (shared_count, PARAMS), jnp.float32)
    common = jnp.dot(coefs, directions) / jnp.sqrt(jnp.float32(shared_count))
    total = (noise + common) * jnp.sqrt(jnp.float32(SAMPLES) / jnp.float32(PARAMS))
    return total.astype(jnp.bfloat16)


def draw_sample_slot(key, part):
    base = jax.random.fold_in(key, 23)

    def one_group(index):
        return jax.random.permutation(jax.random.fold_in(base, index), GROUP).astype(jnp.int32)
    return jax.vmap(one_group)(jnp.arange(GROUPS, dtype=jnp.int32)).reshape(SAMPLES)


def setup_inputs(seed: int = 0) -> dict:
    keys = jax.random.split(jax.random.key(seed), 5)
    jacobian = draw_jacobian(jax.random.fold_in(keys[4], 71), 0)
    sample_slot = draw_sample_slot(jax.random.fold_in(keys[4], 71), 0)
    panel_index = jax.random.randint(keys[2], (1,), 0, SAMPLES).astype(jnp.int32)
    shift_value = jnp.clip(jnp.exp(jax.random.uniform(keys[3], (1,), jnp.float32, math.log(0.1), math.log(1.0))), 0.1, 1.0)
    return {"jacobian": jacobian, "sample_slot": sample_slot, "panel_index": panel_index, "shift_value": shift_value}


def reference(jacobian, sample_slot, panel_index, shift_value):
    grouped = jacobian.reshape(GROUPS, GROUP, PARAMS)
    slots = sample_slot.reshape(GROUPS, GROUP)
    inverse = jnp.argsort(slots, axis=1).astype(jnp.int32)
    ordered = jnp.take_along_axis(grouped, inverse[:, :, None], axis=1)
    pivot_group = panel_index[0] // GROUP
    rotation = panel_index[0] % GROUP
    pivot = jnp.roll(lax.dynamic_index_in_dim(ordered, pivot_group, 0, keepdims=False), -rotation, axis=0)
    identity_matrix = jnp.eye(GROUP, dtype=jnp.float32)
    shifted_eye = jnp.roll(identity_matrix, -rotation, axis=1)
    group_ids = jnp.arange(GROUPS, dtype=jnp.int32)

    def one_block(pair):
        rows, gid = pair
        product = lax.dot_general(rows.astype(jnp.float32), pivot.astype(jnp.float32), (((1,), (1,)), ((), ())), preferred_element_type=jnp.float32)
        on_pivot = (gid == pivot_group).astype(jnp.float32)
        return product / SAMPLES + shift_value[0] * on_pivot * shifted_eye
    gram = lax.map(one_block, (ordered, group_ids))
    block = jnp.roll(lax.dynamic_index_in_dim(gram, pivot_group, 0, keepdims=False), -rotation, axis=0)
    factor = jnp.linalg.cholesky(block)
    inverse_factor = lax.linalg.triangular_solve(factor, identity_matrix, left_side=True, lower=True)
    flat = gram.reshape(SAMPLES, GROUP)
    return lax.dot_general(flat.astype(jnp.float32), inverse_factor.astype(jnp.float32), (((1,), (1,)), ((), ())), precision=lax.Precision.HIGHEST, preferred_element_type=jnp.float32)
```

```python
import functools

import jax
import jax.numpy as jnp
from jax import lax
from jax.experimental import pallas as pl
from jax.experimental.pallas import tpu as pltpu
from jax.sharding import Mesh, PartitionSpec as P

SLAB = ("y", "core", "x")
EVERY = ("y", "core", "z", "x")
CHUNKS = 4
BLOCK = 128
HIGHEST = lax.Precision.HIGHEST


def invert_block(block):
    size = block.shape[0]
    groups = size // 8
    work = [block[8 * h : 8 * h + 8, :] for h in range(groups)]
    lane = lax.broadcasted_iota(jnp.int32, (8, size), 1)
    sub = lax.broadcasted_iota(jnp.int32, (8, size), 0)
    for j in range(size):
        g, s = divmod(j, 8)
        here = lane == j
        columns = [jnp.broadcast_to(work[h][:, j : j + 1], (8, size)) for h in range(g, groups)]
        scale = lax.rsqrt(jnp.broadcast_to(columns[0][s : s + 1, :], (8, size)))
        row = jnp.where(here, 1.0, jnp.broadcast_to(work[g][s : s + 1, :], (8, size))) * scale
        for h in range(g, groups):
            update = jnp.where(here, 0.0, work[h]) - (columns[h - g] * scale) * row
            if h == g:
                update = jnp.where(sub == s, row, jnp.where(sub > s, update, work[h]))
            work[h] = update
    full = jnp.concatenate(work, axis=0)
    rows = lax.broadcasted_iota(jnp.int32, (size, size), 0)
    cols = lax.broadcasted_iota(jnp.int32, (size, size), 1)
    return jnp.where(cols <= rows, full, 0.0)


def inverse_factor_kernel(a_ref, out_ref):
    size = a_ref.shape[0]
    blocks = size // BLOCK
    out_ref[...] = a_ref[...]

    def dot(a, b):
        return jnp.dot(a, b, precision=HIGHEST, preferred_element_type=jnp.float32)

    def step(j, carry):
        here = pl.ds(pl.multiple_of(j * BLOCK, BLOCK), BLOCK)
        inv = invert_block(out_ref[here, here])
        out_ref[here, :] = dot(inv, out_ref[here, :])
        out_ref[here, here] = inv

        def rest(i, carry):
            there = pl.ds(pl.multiple_of(i * BLOCK, BLOCK), BLOCK)
            panel = lax.dot_general(
                out_ref[there, here], inv, (((1,), (1,)), ((), ())),
                precision=HIGHEST, preferred_element_type=jnp.float32,
            )
            out_ref[there, here] = jnp.zeros((BLOCK, BLOCK), jnp.float32)
            out_ref[there, :] -= dot(panel, out_ref[here, :])
            return carry

        return lax.fori_loop(j + 1, blocks, rest, carry)

    lax.fori_loop(0, blocks, step, 0)
    for j in range(blocks - 1):
        out_ref[j * BLOCK : (j + 1) * BLOCK, (j + 1) * BLOCK :] = jnp.zeros(
            (BLOCK, size - (j + 1) * BLOCK), jnp.float32
        )


def inverse_factor_of(block):
    size = block.shape[0]
    return pl.pallas_call(
        inverse_factor_kernel,
        out_shape=jax.ShapeDtypeStruct(block.shape, jnp.float32),
        in_specs=[pl.BlockSpec(memory_space=pltpu.VMEM)],
        out_specs=pl.BlockSpec(memory_space=pltpu.VMEM),
        compiler_params=pltpu.CompilerParams(vmem_limit_bytes=40 * 1024 * 1024),
        cost_estimate=pl.CostEstimate(flops=12 * size**3, bytes_accessed=8 * size**2, transcendentals=size),
        name="inverse_factor",
    )(block)


def thirds(values):
    high = lax.reduce_precision(values, 8, 7)
    rest = values - high
    middle = lax.reduce_precision(rest, 8, 7)
    low = rest - middle
    return [part.astype(jnp.bfloat16) for part in (high, middle, low)]


def dot_last(a, b):
    return lax.dot_general(a, b, (((a.ndim - 1,), (b.ndim - 1,)), ((), ())), preferred_element_type=jnp.float32)


def pick_columns(values, chosen):
    return sum(dot_last(part, chosen) for part in reversed(thirds(values)))


def pick_rows(chosen, values):
    return sum(
        jnp.dot(chosen, part, preferred_element_type=jnp.float32) for part in reversed(thirds(values))
    )


def on_device(jacobian, sample_slot, panel_index, shift_value):
    rows, params = jacobian.shape
    layers = lax.axis_size("z")
    slab = lax.axis_size(SLAB)
    width = lax.axis_size("x") * rows
    group = layers * width
    samples = group * lax.axis_size(("y", "core"))
    pivot_group = panel_index[0] // group
    rotation = panel_index[0] % group
    layer = lax.axis_index("z")
    own_group = lax.axis_index(("y", "core"))
    first_slot = lax.axis_index(("z", "x")) * rows

    slots = lax.all_gather(sample_slot, EVERY, axis=0, tiled=True)
    slots, jacobian = lax.optimization_barrier((slots, jacobian))
    slots = slots.reshape(samples // group, group)

    step = params // CHUNKS
    onward = [(z, (z + 1) % layers) for z in range(layers)]
    totals = [None] * layers
    for chunk in range(CHUNKS):
        piece = lax.slice_in_dim(jacobian, chunk * step, (chunk + 1) * step, axis=1)
        arrived = lax.all_to_all(piece, SLAB, split_axis=1, concat_axis=0, tiled=True)
        pivots = lax.dynamic_slice_in_dim(arrived, pivot_group * width, width, 0)
        for r in range(layers):
            product = dot_last(arrived, pivots)
            totals[r] = product if totals[r] is None else totals[r] + product
            if r + 1 < layers:
                pivots = lax.ppermute(pivots, "z", onward)
    partial = jnp.concatenate(totals, axis=1) / samples

    pivot_slots = lax.dynamic_index_in_dim(slots, pivot_group, 0, keepdims=False)
    column_of = (pivot_slots - rotation) % group
    order = (layer - jnp.arange(layers)) % layers
    near = jnp.take(column_of.reshape(layers, width), order, axis=0).reshape(group)
    index = jnp.arange(group)
    column_pick = (index[:, None] == near[None, :]).astype(jnp.bfloat16)

    pivot_part = lax.dynamic_slice_in_dim(partial, pivot_group * width, width, 0)
    pivot_part = lax.psum_scatter(pivot_part, SLAB, scatter_dimension=0, tiled=True)
    pivot_part = pick_columns(pivot_part, column_pick)
    everyone = lax.all_gather(pivot_part, ("z",) + SLAB, axis=0, tiled=True)
    row_pick = (index[:, None] == column_of[None, :]).astype(jnp.bfloat16)
    block = pick_rows(row_pick, everyone)
    block = block + shift_value[0] * jnp.eye(group, dtype=jnp.float32)
    inverse_factor = inverse_factor_of(block)

    mine = lax.psum_scatter(partial, SLAB, scatter_dimension=0, tiled=True)
    mine = pick_columns(mine, column_pick)
    own = lax.all_gather(mine, ("z", "x"), axis=0, tiled=True)
    own_slots = lax.dynamic_index_in_dim(slots, own_group, 0, keepdims=False)
    out_slots = first_slot + jnp.arange(rows)
    own_pick = (out_slots[:, None] == own_slots[None, :]).astype(jnp.bfloat16)
    gram = pick_rows(own_pick, own)
    on_pivot = (own_group == pivot_group).astype(jnp.float32)
    shifted_eye = ((out_slots - rotation) % group)[:, None] == index[None, :]
    gram = gram + shift_value[0] * on_pivot * shifted_eye.astype(jnp.float32)
    return lax.dot_general(
        gram, inverse_factor, (((1,), (1,)), ((), ())), precision=HIGHEST, preferred_element_type=jnp.float32
    )


def solution(mesh):
    samp, par = mesh.shape["samp"], mesh.shape["par"]
    y = samp // 2
    x = y if par % y == 0 else 1
    fine = Mesh(mesh.devices.reshape(y, 2, par // x, x), EVERY)
    placed = (P(EVERY, None), P(EVERY), P(), P())
    return jax.shard_map(on_device, mesh=fine, in_specs=placed, out_specs=P(EVERY, None), check_vma=False)
```

```python
import itertools
import math

import jax
import jax.numpy as jnp
from jax import lax
from jax.experimental import pallas as pl
from jax.experimental.pallas import tpu as pltpu
from jax.sharding import Mesh, PartitionSpec as P

SLAB = ("y", "core", "x")
EVERY = ("y", "core", "z", "x")
CHUNKS = 4
BLOCK = 128
HIGHEST = lax.Precision.HIGHEST


def invert_block(block):
    size = block.shape[0]
    groups = size // 8
    shape = (8, size)
    work = [block[8 * h : 8 * h + 8, :] for h in range(groups)]
    lane = lax.broadcasted_iota(jnp.int32, shape, 1)
    sub = lax.broadcasted_iota(jnp.int32, shape, 0)

    def column(h, j):
        return jnp.broadcast_to(work[h][:, j : j + 1], shape)

    def total(terms):
        while len(terms) > 1:
            terms = [sum(terms[i + 1 : i + 2], terms[i]) for i in range(0, len(terms), 2)]
        return terms[0]

    for g in range(groups):
        first = 8 * g
        inside = (lane >= first) & (lane < first + 8)
        diagonal = [column(g, first + j) for j in range(8)]
        swept = {(i, j): jnp.broadcast_to(diagonal[j][i : i + 1, :], shape) for i in range(8) for j in range(i + 1)}
        current = jnp.where(inside, (lane - first == sub).astype(jnp.float32), work[g])
        rows = [jnp.broadcast_to(current[i : i + 1, :], shape) for i in range(8)]
        inverse = {}

        def at(k, j):
            return (k, j) if k >= j else (j, k)

        for i in range(8):
            root = lax.rsqrt(swept[i, i])
            reciprocal = root * root
            inverse[i, i] = root
            for j in range(i):
                inverse[i, j] = -swept[i, j] * root
            old = {k: swept[at(k, i)] for k in range(8) if k != i}
            scaled = {k: old[k] * reciprocal for k in old}
            for k in old:
                for j in old:
                    if j <= k:
                        swept[k, j] = swept[k, j] - old[k] * scaled[j]
                swept[at(k, i)] = scaled[k]
            swept[i, i] = -reciprocal
        combined = [total([swept[at(j, i)] * rows[i] for i in range(8)]) for j in range(8)]
        for h in range(g + 1, groups):
            terms = [column(h, first + j) * combined[j] for j in range(8)]
            work[h] = total([jnp.where(inside, 0.0, work[h])] + terms)
        done = None
        for i in range(8):
            row = total([inverse[i, j] * rows[j] for j in range(i + 1)])
            done = row if done is None else jnp.where(sub == i, row, done)
        work[g] = done
    full = jnp.concatenate(work, axis=0)
    row_of = lax.broadcasted_iota(jnp.int32, (size, size), 0)
    column_of = lax.broadcasted_iota(jnp.int32, (size, size), 1)
    return jnp.where(column_of <= row_of, full, 0.0)


def three_parts(values):
    high = values.astype(jnp.bfloat16)
    rest = values - high.astype(jnp.float32)
    middle = rest.astype(jnp.bfloat16)
    low = (rest - middle.astype(jnp.float32)).astype(jnp.bfloat16)
    return high, middle, low


def left_parts(values):
    high, middle, low = three_parts(values)
    return jnp.concatenate([high, high, middle, middle, high, low], axis=1)


def right_parts(values):
    high, middle, low = three_parts(values)
    return jnp.concatenate([high, middle, high, middle, low, high], axis=0)


def inverse_factor_kernel(a_ref, out_ref, parts_ref):
    size = a_ref.shape[0]
    blocks = size // BLOCK
    out_ref[...] = a_ref[...]

    def dot(left, right):
        return jnp.dot(left, right, preferred_element_type=jnp.float32)

    def step(j, carry):
        here = pl.ds(pl.multiple_of(j * BLOCK, BLOCK), BLOCK)
        inv = invert_block(out_ref[here, here])
        parts_ref[...] = right_parts(out_ref[here, :])
        out_ref[here, :] = dot(left_parts(inv), parts_ref[...])
        out_ref[here, here] = inv
        parts_ref[...] = right_parts(out_ref[here, :])
        across = right_parts(inv.T)

        def rest(i, carry):
            there = pl.ds(pl.multiple_of(i * BLOCK, BLOCK), BLOCK)
            panel = dot(left_parts(out_ref[there, here]), across)
            out_ref[there, here] = jnp.zeros((BLOCK, BLOCK), jnp.float32)
            out_ref[there, :] -= dot(left_parts(panel), parts_ref[...])
            return carry

        return lax.fori_loop(j + 1, blocks, rest, carry)

    lax.fori_loop(0, blocks, step, 0)
    for j in range(blocks - 1):
        out_ref[j * BLOCK : (j + 1) * BLOCK, (j + 1) * BLOCK :] = jnp.zeros(
            (BLOCK, size - (j + 1) * BLOCK), jnp.float32
        )


def inverse_factor_of(block):
    size = block.shape[0]
    return pl.pallas_call(
        inverse_factor_kernel,
        out_shape=jax.ShapeDtypeStruct(block.shape, jnp.float32),
        in_specs=[pl.BlockSpec(memory_space=pltpu.VMEM)],
        out_specs=pl.BlockSpec(memory_space=pltpu.VMEM),
        scratch_shapes=[pltpu.VMEM((6 * BLOCK, size), jnp.bfloat16)],
        compiler_params=pltpu.CompilerParams(vmem_limit_bytes=40 * 1024 * 1024),
        cost_estimate=pl.CostEstimate(flops=12 * size**3, bytes_accessed=8 * size**2, transcendentals=size),
        name="inverse_factor",
    )(block)


def thirds(values):
    high = lax.reduce_precision(values, 8, 7)
    rest = values - high
    middle = lax.reduce_precision(rest, 8, 7)
    low = rest - middle
    return [part.astype(jnp.bfloat16) for part in (high, middle, low)]


def dot_last(a, b):
    return lax.dot_general(a, b, (((a.ndim - 1,), (b.ndim - 1,)), ((), ())), preferred_element_type=jnp.float32)


def pick_columns(values, chosen):
    return sum(dot_last(part, chosen) for part in reversed(thirds(values)))


def pick_rows(chosen, values):
    return sum(
        jnp.dot(chosen, part, preferred_element_type=jnp.float32) for part in reversed(thirds(values))
    )


def ring_gather(values, axis):
    count = lax.axis_size(axis)
    rows = values.shape[0]
    here = lax.axis_index(axis)
    whole = jnp.zeros((count * rows,) + values.shape[1:], values.dtype)
    onward = [(i, (i + 1) % count) for i in range(count)]
    for step in range(count):
        whole = lax.dynamic_update_slice_in_dim(whole, values, (here - step) % count * rows, 0)
        if step + 1 < count:
            values = lax.ppermute(values, axis, onward)
    return whole


def exchange_tiles(piece):
    sizes = [lax.axis_size(axis) for axis in SLAB]
    own = [lax.axis_index(axis) for axis in SLAB]
    count = math.prod(sizes)
    rows, width = piece.shape[0], piece.shape[1] // count

    def flat(place):
        index = 0
        for size, coordinate in zip(sizes, place):
            index = index * size + coordinate % size
        return index

    places = list(itertools.product(*(range(size) for size in sizes)))
    whole = jnp.zeros((count * rows, width), piece.dtype)
    parts = []
    for offset in places:
        target = flat([c + o for c, o in zip(own, offset)])
        part = lax.dynamic_slice_in_dim(piece, target * width, width, 1)
        if any(offset):
            pairs = [(flat(p), flat([c + o for c, o in zip(p, offset)])) for p in places]
            part = lax.ppermute(part, SLAB, pairs)
        parts.append((flat([c - o for c, o in zip(own, offset)]), part))
    for source, part in parts:
        whole = lax.dynamic_update_slice_in_dim(whole, part, source * rows, 0)
    return whole


def on_device(jacobian, sample_slot, panel_index, shift_value):
    rows, params = jacobian.shape
    layers = lax.axis_size("z")
    slab = lax.axis_size(SLAB)
    width = lax.axis_size("x") * rows
    group = layers * width
    samples = group * lax.axis_size(("y", "core"))
    pivot_group = panel_index[0] // group
    rotation = panel_index[0] % group
    layer = lax.axis_index("z")
    own_group = lax.axis_index(("y", "core"))
    first_slot = lax.axis_index(("z", "x")) * rows

    slots = sample_slot[None]
    for axis in reversed(EVERY):
        slots = ring_gather(slots, axis)
    slots = slots.reshape(samples // group, group)

    step = params // CHUNKS
    onward = [(z, (z + 1) % layers) for z in range(layers)]
    totals = [None] * layers
    arrived = None
    for chunk in range(CHUNKS):
        piece = lax.slice_in_dim(jacobian, chunk * step, (chunk + 1) * step, axis=1)
        if arrived is not None:
            piece, arrived = lax.optimization_barrier((piece, arrived))
        arrived = exchange_tiles(piece)
        pivots = lax.dynamic_slice_in_dim(arrived, pivot_group * width, width, 0)
        for r in range(layers):
            product = dot_last(arrived, pivots)
            totals[r] = product if totals[r] is None else totals[r] + product
            if r + 1 < layers:
                pivots = lax.ppermute(pivots, "z", onward)
    partial = jnp.concatenate(totals, axis=1) / samples

    pivot_slots = lax.dynamic_index_in_dim(slots, pivot_group, 0, keepdims=False)
    column_of = (pivot_slots - rotation) % group
    order = (layer - jnp.arange(layers)) % layers
    near = jnp.take(column_of.reshape(layers, width), order, axis=0).reshape(group)
    index = jnp.arange(group)
    column_pick = (index[:, None] == near[None, :]).astype(jnp.bfloat16)

    pivot_part = lax.dynamic_slice_in_dim(partial, pivot_group * width, width, 0)
    pivot_part = lax.psum_scatter(pivot_part, SLAB, scatter_dimension=0, tiled=True)
    pivot_part = pick_columns(pivot_part, column_pick)
    everyone = lax.all_gather(pivot_part, ("z",) + SLAB, axis=0, tiled=True)
    row_pick = (index[:, None] == column_of[None, :]).astype(jnp.bfloat16)
    block = pick_rows(row_pick, everyone)
    block = block + shift_value[0] * jnp.eye(group, dtype=jnp.float32)

    partial, block = lax.optimization_barrier((partial, block))
    mine = lax.psum_scatter(partial, SLAB, scatter_dimension=0, tiled=True)
    inverse_factor = inverse_factor_of(block)
    mine = pick_columns(mine, column_pick)
    own = lax.all_gather(mine, ("z", "x"), axis=0, tiled=True)
    own_slots = lax.dynamic_index_in_dim(slots, own_group, 0, keepdims=False)
    out_slots = first_slot + jnp.arange(rows)
    own_pick = (out_slots[:, None] == own_slots[None, :]).astype(jnp.bfloat16)
    gram = pick_rows(own_pick, own)
    on_pivot = (own_group == pivot_group).astype(jnp.float32)
    shifted_eye = ((out_slots - rotation) % group)[:, None] == index[None, :]
    gram = gram + shift_value[0] * on_pivot * shifted_eye.astype(jnp.float32)
    return lax.dot_general(
        gram, inverse_factor, (((1,), (1,)), ((), ())), precision=HIGHEST, preferred_element_type=jnp.float32
    )


def solution(mesh):
    samp, par = mesh.shape["samp"], mesh.shape["par"]
    y = samp // 2
    x = y if par % y == 0 else 1
    fine = Mesh(mesh.devices.reshape(y, 2, par // x, x), EVERY)
    placed = (P(EVERY, None), P(EVERY), P(), P())
    return jax.shard_map(on_device, mesh=fine, in_specs=placed, out_specs=P(EVERY, None), check_vma=False)
```

```python
import jax
import jax.numpy as jnp
from jax import lax
from jax.experimental import pallas as pl
from jax.experimental.pallas import tpu as pltpu
from jax.sharding import Mesh, PartitionSpec as P

SLAB = ("y", "core", "x")
EVERY = ("y", "core", "z", "x")
SHARES = (2, 4, 5, 5)
BLOCK = 128
HIGHEST = lax.Precision.HIGHEST


def invert_block(block):
    size = block.shape[0]
    groups = size // 8
    shape = (8, size)
    work = [block[8 * h : 8 * h + 8, :] for h in range(groups)]
    lane = lax.broadcasted_iota(jnp.int32, shape, 1)
    sub = lax.broadcasted_iota(jnp.int32, shape, 0)

    def column(h, j):
        return jnp.broadcast_to(work[h][:, j : j + 1], shape)

    def total(terms):
        while len(terms) > 1:
            terms = [sum(terms[i + 1 : i + 2], terms[i]) for i in range(0, len(terms), 2)]
        return terms[0]

    for g in range(groups):
        first = 8 * g
        inside = (lane >= first) & (lane < first + 8)
        diagonal = [column(g, first + j) for j in range(8)]
        swept = {(i, j): jnp.broadcast_to(diagonal[j][i : i + 1, :], shape) for i in range(8) for j in range(i + 1)}
        current = jnp.where(inside, (lane - first == sub).astype(jnp.float32), work[g])
        rows = [jnp.broadcast_to(current[i : i + 1, :], shape) for i in range(8)]
        inverse = {}

        def at(k, j):
            return (k, j) if k >= j else (j, k)

        for i in range(8):
            root = lax.rsqrt(swept[i, i])
            reciprocal = root * root
            inverse[i, i] = root
            for j in range(i):
                inverse[i, j] = -swept[i, j] * root
            old = {k: swept[at(k, i)] for k in range(8) if k != i}
            scaled = {k: old[k] * reciprocal for k in old}
            for k in old:
                for j in old:
                    if j <= k:
                        swept[k, j] = swept[k, j] - old[k] * scaled[j]
                swept[at(k, i)] = scaled[k]
            swept[i, i] = -reciprocal
        combined = [total([swept[at(j, i)] * rows[i] for i in range(8)]) for j in range(8)]
        for h in range(g + 1, groups):
            terms = [column(h, first + j) * combined[j] for j in range(8)]
            work[h] = total([jnp.where(inside, 0.0, work[h])] + terms)
        done = None
        for i in range(8):
            row = total([inverse[i, j] * rows[j] for j in range(i + 1)])
            done = row if done is None else jnp.where(sub == i, row, done)
        work[g] = done
    full = jnp.concatenate(work, axis=0)
    row_of = lax.broadcasted_iota(jnp.int32, (size, size), 0)
    column_of = lax.broadcasted_iota(jnp.int32, (size, size), 1)
    return jnp.where(column_of <= row_of, full, 0.0)


def three_parts(values):
    high = values.astype(jnp.bfloat16)
    rest = values - high.astype(jnp.float32)
    middle = rest.astype(jnp.bfloat16)
    low = (rest - middle.astype(jnp.float32)).astype(jnp.bfloat16)
    return high, middle, low


def left_parts(values):
    high, middle, low = three_parts(values)
    return jnp.concatenate([high, high, middle, middle, high, low], axis=1)


def right_parts(values):
    high, middle, low = three_parts(values)
    return jnp.concatenate([high, middle, high, middle, low, high], axis=0)


def inverse_factor_kernel(a_ref, out_ref, parts_ref):
    size = a_ref.shape[0]
    blocks = size // BLOCK
    out_ref[...] = a_ref[...]

    def dot(left, right):
        return jnp.dot(left, right, preferred_element_type=jnp.float32)

    def step(j, carry):
        here = pl.ds(pl.multiple_of(j * BLOCK, BLOCK), BLOCK)
        inv = invert_block(out_ref[here, here])
        parts_ref[...] = right_parts(out_ref[here, :])
        out_ref[here, :] = dot(left_parts(inv), parts_ref[...])
        out_ref[here, here] = inv
        parts_ref[...] = right_parts(out_ref[here, :])
        across = right_parts(inv.T)

        def rest(i, carry):
            there = pl.ds(pl.multiple_of(i * BLOCK, BLOCK), BLOCK)
            panel = dot(left_parts(out_ref[there, here]), across)
            out_ref[there, here] = jnp.zeros((BLOCK, BLOCK), jnp.float32)
            out_ref[there, :] -= dot(left_parts(panel), parts_ref[...])
            return carry

        return lax.fori_loop(j + 1, blocks, rest, carry)

    lax.fori_loop(0, blocks, step, 0)
    for j in range(blocks - 1):
        out_ref[j * BLOCK : (j + 1) * BLOCK, (j + 1) * BLOCK :] = jnp.zeros(
            (BLOCK, size - (j + 1) * BLOCK), jnp.float32
        )


def inverse_factor_of(block):
    size = block.shape[0]
    return pl.pallas_call(
        inverse_factor_kernel,
        out_shape=jax.ShapeDtypeStruct(block.shape, jnp.float32),
        in_specs=[pl.BlockSpec(memory_space=pltpu.VMEM)],
        out_specs=pl.BlockSpec(memory_space=pltpu.VMEM),
        scratch_shapes=[pltpu.VMEM((6 * BLOCK, size), jnp.bfloat16)],
        compiler_params=pltpu.CompilerParams(vmem_limit_bytes=40 * 1024 * 1024),
        cost_estimate=pl.CostEstimate(flops=12 * size**3, bytes_accessed=8 * size**2, transcendentals=size),
        name="inverse_factor",
    )(block)


def thirds(values):
    high = lax.reduce_precision(values, 8, 7)
    rest = values - high
    middle = lax.reduce_precision(rest, 8, 7)
    low = rest - middle
    return [part.astype(jnp.bfloat16) for part in (high, middle, low)]


def dot_last(a, b):
    return lax.dot_general(a, b, (((a.ndim - 1,), (b.ndim - 1,)), ((), ())), preferred_element_type=jnp.float32)


def pick_columns(values, chosen):
    return sum(dot_last(part, chosen) for part in reversed(thirds(values)))


def pick_rows(chosen, values):
    return sum(
        jnp.dot(chosen, part, preferred_element_type=jnp.float32) for part in reversed(thirds(values))
    )


def onward(axis, offset):
    count = lax.axis_size(axis)
    return [(i, (i + offset) % count) for i in range(count)]


def gather(values, axis):
    count = lax.axis_size(axis)
    return jnp.stack([values] + [lax.ppermute(values, axis, onward(axis, o)) for o in range(1, count)])


def before(axis):
    count = lax.axis_size(axis)
    return (lax.axis_index(axis) - jnp.arange(count)) % count


def split_columns(values, axis):
    count = lax.axis_size(axis)
    here = lax.axis_index(axis)
    width = values.shape[-1] // count
    parts = []
    for offset in range(count):
        part = lax.dynamic_slice_in_dim(values, (here + offset) % count * width, width, values.ndim - 1)
        parts.append(lax.ppermute(part, axis, onward(axis, offset)) if offset else part)
    return jnp.stack(parts)


def exchange_tiles(piece):
    shared = split_columns(piece, "core")
    half = shared.shape[-1] // 2
    one = split_columns(split_columns(shared[..., :half], "x"), "y")
    two = split_columns(split_columns(shared[..., half:], "y"), "x")
    return jnp.concatenate([one, jnp.swapaxes(two, 0, 1)], axis=-1)


def on_device(jacobian, sample_slot, panel_index, shift_value):
    rows, params = jacobian.shape
    sizes = {axis: lax.axis_size(axis) for axis in EVERY}
    own = {axis: lax.axis_index(axis) for axis in EVERY}
    layers, across = sizes["z"], sizes["x"]
    slab = lax.axis_size(SLAB)
    width = across * rows
    group = layers * width
    members = layers * across
    samples = group * sizes["y"] * sizes["core"]
    pivot_group = panel_index[0] // group
    rotation = panel_index[0] % group
    own_group = lax.axis_index(("y", "core"))
    member = lax.axis_index(("z", "x"))

    slots = sample_slot
    for axis in reversed(EVERY):
        slots = gather(slots, axis)
    for dim, axis in enumerate(EVERY):
        slots = jnp.take(slots, before(axis), axis=dim)
    slots = slots.reshape(samples // group, group)

    pivot_y = (own["y"] - pivot_group // sizes["core"]) % sizes["y"]
    pivot_core = (own["core"] - pivot_group % sizes["core"]) % sizes["core"]
    totals = [None] * layers
    arrived = None
    start = 0
    for chunk, share in enumerate(SHARES):
        step = params * share // sum(SHARES)
        piece = lax.slice_in_dim(jacobian, start, start + step, axis=1)
        start += step
        if chunk == 1:
            piece, slots = lax.optimization_barrier((piece, slots))
        if arrived is not None:
            piece, arrived = lax.optimization_barrier((piece, arrived))
        arrived = exchange_tiles(piece)
        pivots = lax.dynamic_index_in_dim(arrived, pivot_y, 0, keepdims=False)
        pivots = lax.dynamic_index_in_dim(pivots, pivot_core, 1, keepdims=False)
        pivots = jnp.take(pivots, before("x"), axis=0).reshape(width, step // slab)
        samples_here = arrived.reshape(slab * rows, step // slab)
        for r in range(layers):
            product = dot_last(samples_here, pivots)
            totals[r] = product if totals[r] is None else totals[r] + product
            if r + 1 < layers:
                pivots = lax.ppermute(pivots, "z", onward("z", 1))
    partial = (jnp.concatenate(totals, axis=1) / samples).reshape(sizes["y"], across, sizes["core"], rows, group)

    pivot_slots = lax.dynamic_index_in_dim(slots, pivot_group, 0, keepdims=False)
    column_of = (pivot_slots - rotation) % group
    near = jnp.take(column_of.reshape(layers, width), before("z"), axis=0).reshape(group)
    index = jnp.arange(group)
    column_pick = (index[:, None] == near[None, :]).astype(jnp.bfloat16)

    pivot_part = lax.dynamic_index_in_dim(partial, pivot_y, 0, keepdims=False)
    pivot_part = lax.dynamic_index_in_dim(pivot_part, pivot_core, 1, keepdims=False)
    pivot_part = jnp.take(pivot_part, before("x"), axis=0).reshape(width, group)
    pivot_part = lax.psum_scatter(pivot_part, SLAB, scatter_dimension=0, tiled=True)
    partial, pivot_part = lax.optimization_barrier((partial, pivot_part))
    pivot_part = pick_columns(pivot_part, column_pick)
    part_rows = width // slab
    half = group // 2
    layered = gather(pivot_part, "z")
    halves = []
    for values, first, second in ((layered[..., :half], "x", "y"), (layered[..., half:], "y", "x")):
        values = gather(gather(values, first), second)
        others = [values] + [lax.ppermute(values, "core", onward("core", o)) for o in range(1, sizes["core"])]
        places = column_of.reshape(layers, sizes["y"], sizes["core"], across, part_rows)
        for dim, axis in enumerate(("z", "y", "core", "x")):
            places = jnp.take(places, before(axis), axis=dim)
        order = {"z": 0, "y": 1, "core": 2, "x": 3}
        places = places.transpose(order["core"], order[second], order[first], order["z"], 4)
        picked = None
        for o, other in enumerate(others):
            row_pick = (index[:, None] == places[o].reshape(-1)[None, :]).astype(jnp.bfloat16)
            part = pick_rows(row_pick, other.reshape(-1, half))
            picked = part if picked is None else picked + part
        halves.append(picked)
    block = jnp.concatenate(halves, axis=1) + shift_value[0] * jnp.eye(group, dtype=jnp.float32)

    mine = jnp.take(partial, before("y"), axis=0)
    mine = jnp.take(mine, before("x"), axis=1)
    mine = jnp.take(mine, before("core"), axis=2)
    mine = mine.transpose(0, 2, 1, 3, 4).reshape(slab * rows, group)
    mine = lax.psum_scatter(mine, SLAB, scatter_dimension=0, tiled=True)
    mine = pick_columns(mine, column_pick)

    room = 8 * -(-5 * rows // 128)
    owners = (slots // rows).reshape(-1, members, rows)
    earlier = jnp.arange(rows)[:, None] > jnp.arange(rows)[None, :]
    alike = owners[..., :, None] == owners[..., None, :]
    rank = jnp.sum(alike & earlier, axis=-1)
    rounds = jnp.max(rank) // room + 1
    own_slots = lax.dynamic_index_in_dim(slots, own_group, 0, keepdims=False).reshape(members, rows)
    own_owners = lax.dynamic_index_in_dim(owners, own_group, 0, keepdims=False)
    own_rank = lax.dynamic_index_in_dim(rank, own_group, 0, keepdims=False)
    steps = [(a, b) for a in range(layers) for b in range(across)]
    places = [(a, b) for a in range(layers) for b in range(across)]

    def moved(a, b):
        return (a % layers) * across + b % across

    def exchange_rows(number, rows_here):
        seat = number * room + jnp.arange(room)
        sent = []
        for a, b in steps:
            target = moved(own["z"] + a, own["x"] + b)
            goes = (own_owners[member] == target)[None, :] & (own_rank[member][None, :] == seat[:, None])
            sent.append(goes)
        sent = pick_rows(jnp.concatenate(sent).astype(jnp.bfloat16), rows_here)
        received, names = [], []
        for i, (a, b) in enumerate(steps):
            part = sent[i * room : (i + 1) * room]
            if (a, b) != (0, 0):
                pairs = [(moved(*p), moved(p[0] + a, p[1] + b)) for p in places]
                part = lax.ppermute(part, ("z", "x"), pairs)
            source = moved(own["z"] - a, own["x"] - b)
            comes = (own_owners[source] == member)[None, :] & (own_rank[source][None, :] == seat[:, None])
            received.append(part)
            names.append(jnp.max(jnp.where(comes, own_slots[source][None, :], -1), axis=1))
        out_slots = member * rows + jnp.arange(rows)
        pick = out_slots[:, None] == jnp.concatenate(names)[None, :]
        return pick_rows(pick.astype(jnp.bfloat16), jnp.concatenate(received))

    gram = exchange_rows(0, mine)
    inverse_factor = inverse_factor_of(block)
    gram = lax.fori_loop(1, rounds, lambda number, total: total + exchange_rows(number, mine), gram)
    on_pivot = (own_group == pivot_group).astype(jnp.float32)
    out_slots = member * rows + jnp.arange(rows)
    shifted_eye = ((out_slots - rotation) % group)[:, None] == index[None, :]
    gram = gram + shift_value[0] * on_pivot * shifted_eye.astype(jnp.float32)
    return lax.dot_general(
        gram, inverse_factor, (((1,), (1,)), ((), ())), precision=HIGHEST, preferred_element_type=jnp.float32
    )


def solution(mesh):
    samp, par = mesh.shape["samp"], mesh.shape["par"]
    y = samp // 2
    x = y if par % y == 0 else 1
    fine = Mesh(mesh.devices.reshape(y, 2, par // x, x), EVERY)
    placed = (P(EVERY, None), P(EVERY), P(), P())
    return jax.shard_map(on_device, mesh=fine, in_specs=placed, out_specs=P(EVERY, None), check_vma=False)
```

```python
import jax
import jax.numpy as jnp
from jax import lax
from jax.experimental import pallas as pl
from jax.experimental.pallas import tpu as pltpu
from jax.sharding import Mesh, PartitionSpec as P

SLAB = ("y", "core", "x")
EVERY = ("y", "core", "z", "x")
SHARES = (2, 3, 4, 4, 3)
BLOCK = 128
HIGHEST = lax.Precision.HIGHEST


def invert_block(block):
    size = block.shape[0]
    groups = size // 8
    shape = (8, size)
    work = [block[8 * h : 8 * h + 8, :] for h in range(groups)]
    lane = lax.broadcasted_iota(jnp.int32, shape, 1)
    sub = lax.broadcasted_iota(jnp.int32, shape, 0)

    def column(h, j):
        return jnp.broadcast_to(work[h][:, j : j + 1], shape)

    def total(terms):
        while len(terms) > 1:
            terms = [sum(terms[i + 1 : i + 2], terms[i]) for i in range(0, len(terms), 2)]
        return terms[0]

    for g in range(groups):
        first = 8 * g
        inside = (lane >= first) & (lane < first + 8)
        diagonal = [column(g, first + j) for j in range(8)]
        swept = {(i, j): jnp.broadcast_to(diagonal[j][i : i + 1, :], shape) for i in range(8) for j in range(i + 1)}
        current = jnp.where(inside, (lane - first == sub).astype(jnp.float32), work[g])
        rows = [jnp.broadcast_to(current[i : i + 1, :], shape) for i in range(8)]
        inverse = {}

        def at(k, j):
            return (k, j) if k >= j else (j, k)

        for i in range(8):
            root = lax.rsqrt(swept[i, i])
            reciprocal = root * root
            inverse[i, i] = root
            for j in range(i):
                inverse[i, j] = -swept[i, j] * root
            old = {k: swept[at(k, i)] for k in range(8) if k != i}
            scaled = {k: old[k] * reciprocal for k in old}
            for k in old:
                for j in old:
                    if j <= k:
                        swept[k, j] = swept[k, j] - old[k] * scaled[j]
                swept[at(k, i)] = scaled[k]
            swept[i, i] = -reciprocal
        combined = [total([swept[at(j, i)] * rows[i] for i in range(8)]) for j in range(8)]
        for h in range(g + 1, groups):
            terms = [column(h, first + j) * combined[j] for j in range(8)]
            work[h] = total([jnp.where(inside, 0.0, work[h])] + terms)
        done = None
        for i in range(8):
            row = total([inverse[i, j] * rows[j] for j in range(i + 1)])
            done = row if done is None else jnp.where(sub == i, row, done)
        work[g] = done
    full = jnp.concatenate(work, axis=0)
    row_of = lax.broadcasted_iota(jnp.int32, (size, size), 0)
    column_of = lax.broadcasted_iota(jnp.int32, (size, size), 1)
    return jnp.where(column_of <= row_of, full, 0.0)


def three_parts(values):
    high = values.astype(jnp.bfloat16)
    rest = values - high.astype(jnp.float32)
    middle = rest.astype(jnp.bfloat16)
    low = (rest - middle.astype(jnp.float32)).astype(jnp.bfloat16)
    return high, middle, low


def left_parts(values):
    high, middle, low = three_parts(values)
    return jnp.concatenate([high, high, middle, middle, high, low], axis=1)


def right_parts(values):
    high, middle, low = three_parts(values)
    return jnp.concatenate([high, middle, high, middle, low, high], axis=0)


def inverse_factor_kernel(shift_ref, packed_ref, out_ref, parts_ref):
    size = out_ref.shape[0]
    blocks = size // BLOCK
    band = packed_ref.shape[1] - size
    count = size // band
    out_ref[...] = jnp.zeros(out_ref.shape, jnp.float32)
    for b in range(count // 2):
        c = count - 1 - b
        out_ref[b * band : (b + 1) * band, b * band :] = packed_ref[b * band : (b + 1) * band, : size - b * band]
        out_ref[c * band : (c + 1) * band, c * band :] = packed_ref[b * band : (b + 1) * band, size - b * band :]
    unit = lax.broadcasted_iota(jnp.int32, (BLOCK, BLOCK), 0) == lax.broadcasted_iota(jnp.int32, (BLOCK, BLOCK), 1)

    def dot(left, right):
        return jnp.dot(left, right, preferred_element_type=jnp.float32)

    def step(j, carry):
        here = pl.ds(pl.multiple_of(j * BLOCK, BLOCK), BLOCK)
        inv = invert_block(out_ref[here, here] + jnp.where(unit, shift_ref[0], 0.0))
        parts_ref[...] = right_parts(out_ref[here, :])
        out_ref[here, :] = dot(left_parts(inv), parts_ref[...])
        out_ref[here, here] = inv
        parts_ref[...] = right_parts(out_ref[here, :])

        def rest(i, carry):
            there = pl.ds(pl.multiple_of(i * BLOCK, BLOCK), BLOCK)
            panel = out_ref[here, there].T
            out_ref[there, here] = jnp.zeros((BLOCK, BLOCK), jnp.float32)
            out_ref[there, :] -= dot(left_parts(panel), parts_ref[...])
            return carry

        return lax.fori_loop(j + 1, blocks, rest, carry)

    lax.fori_loop(0, blocks, step, 0)
    for j in range(blocks - 1):
        out_ref[j * BLOCK : (j + 1) * BLOCK, (j + 1) * BLOCK :] = jnp.zeros(
            (BLOCK, size - (j + 1) * BLOCK), jnp.float32
        )


def inverse_factor_of(shift, packed, size):
    return pl.pallas_call(
        inverse_factor_kernel,
        out_shape=jax.ShapeDtypeStruct((size, size), jnp.float32),
        in_specs=[pl.BlockSpec(memory_space=pltpu.SMEM), pl.BlockSpec(memory_space=pltpu.VMEM)],
        out_specs=pl.BlockSpec(memory_space=pltpu.VMEM),
        scratch_shapes=[pltpu.VMEM((6 * BLOCK, size), jnp.bfloat16)],
        compiler_params=pltpu.CompilerParams(vmem_limit_bytes=40 * 1024 * 1024),
        cost_estimate=pl.CostEstimate(flops=12 * size**3, bytes_accessed=8 * size**2, transcendentals=size),
        name="inverse_factor",
    )(shift, packed)


def thirds(values):
    high = lax.reduce_precision(values, 8, 7)
    rest = values - high
    middle = lax.reduce_precision(rest, 8, 7)
    low = rest - middle
    return [part.astype(jnp.bfloat16) for part in (high, middle, low)]


def dot_last(a, b):
    return lax.dot_general(a, b, (((a.ndim - 1,), (b.ndim - 1,)), ((), ())), preferred_element_type=jnp.float32)


def pick_rows(chosen, values):
    return sum(
        jnp.dot(chosen, part, preferred_element_type=jnp.float32) for part in reversed(thirds(values))
    )


def onward(axis, offset):
    count = lax.axis_size(axis)
    return [(i, (i + offset) % count) for i in range(count)]


def gather(values, axis):
    count = lax.axis_size(axis)
    return jnp.stack([values] + [lax.ppermute(values, axis, onward(axis, o)) for o in range(1, count)])


def before(axis):
    count = lax.axis_size(axis)
    return (lax.axis_index(axis) - jnp.arange(count)) % count


def on_device(jacobian, sample_slot, panel_index, shift_value):
    rows, params = jacobian.shape
    sizes = {axis: lax.axis_size(axis) for axis in EVERY}
    own = {axis: lax.axis_index(axis) for axis in EVERY}
    layers, across = sizes["z"], sizes["x"]
    slab = lax.axis_size(SLAB)
    width = across * rows
    group = layers * width
    members = layers * across
    samples = group * sizes["y"] * sizes["core"]
    pivot_group = panel_index[0] // group
    rotation = panel_index[0] % group
    own_group = lax.axis_index(("y", "core"))
    member = lax.axis_index(("z", "x"))

    tiles, pivots = [], []
    start = 0
    for share in SHARES:
        step = params * share // sum(SHARES)
        if tiles:
            jacobian, tiles[-1] = lax.optimization_barrier((jacobian, tiles[-1]))
        piece = lax.slice_in_dim(jacobian, start, start + step, axis=1)
        start += step
        tiles.append(lax.all_to_all(piece, SLAB, split_axis=1, concat_axis=0, tiled=True))
        near = lax.dynamic_slice_in_dim(tiles[-1], pivot_group * width, width, 0)
        pivots.append(lax.all_gather(near, "z", axis=0, tiled=True))

    slots, tiles[-1] = lax.optimization_barrier((sample_slot, tiles[-1]))
    for axis in reversed(EVERY):
        slots = gather(slots, axis)
    for dim, axis in enumerate(EVERY):
        slots = jnp.take(slots, before(axis), axis=dim)
    slots = slots.reshape(samples // group, group)
    pivot_slots = lax.dynamic_index_in_dim(slots, pivot_group, 0, keepdims=False)
    index = jnp.arange(group)
    pick = (index[:, None] == ((pivot_slots - rotation) % group)[None, :]).astype(jnp.bfloat16)

    band = group // (2 * layers)
    low, high = own["z"] * band, (2 * layers - 1 - own["z"]) * band
    panel = lower = upper = 0.0
    for tile, gathered in zip(tiles, pivots):
        ordered = jnp.dot(pick, gathered, preferred_element_type=jnp.float32).astype(jnp.bfloat16)
        panel = panel + dot_last(tile, ordered)
        lower = lower + dot_last(lax.dynamic_slice_in_dim(ordered, low, band, 0), ordered)
        upper = upper + dot_last(lax.dynamic_slice_in_dim(ordered, high, band, 0), ordered)

    place = jnp.arange(group + band)[None, :]
    lower = lax.dynamic_slice_in_dim(jnp.pad(lower, ((0, 0), (0, group))), low, group + band, 1)
    upper = jnp.pad(upper, ((0, 0), (band, 0)))
    packed = jnp.where(place < group - low, lower, upper) / samples
    packed = lax.psum_scatter(packed, SLAB, scatter_dimension=0, tiled=True)
    packed = lax.all_gather(packed, ("z",) + SLAB, axis=0, tiled=True)

    panel, packed = lax.optimization_barrier((panel, packed))
    mine = lax.psum_scatter(panel / samples, SLAB, scatter_dimension=0, tiled=True)

    room = 8 * -(-5 * rows // 128)
    owners = (slots // rows).reshape(-1, members, rows)
    earlier = jnp.arange(rows)[:, None] > jnp.arange(rows)[None, :]
    alike = owners[..., :, None] == owners[..., None, :]
    rank = jnp.sum(alike & earlier, axis=-1)
    rounds = jnp.max(rank) // room + 1
    own_slots = lax.dynamic_index_in_dim(slots, own_group, 0, keepdims=False).reshape(members, rows)
    own_owners = lax.dynamic_index_in_dim(owners, own_group, 0, keepdims=False)
    own_rank = lax.dynamic_index_in_dim(rank, own_group, 0, keepdims=False)
    steps = [(a, b) for a in range(layers) for b in range(across)]
    places = [(a, b) for a in range(layers) for b in range(across)]

    def moved(a, b):
        return (a % layers) * across + b % across

    def exchange_rows(number, rows_here):
        seat = number * room + jnp.arange(room)
        sent = []
        for a, b in steps:
            target = moved(own["z"] + a, own["x"] + b)
            goes = (own_owners[member] == target)[None, :] & (own_rank[member][None, :] == seat[:, None])
            sent.append(goes)
        sent = pick_rows(jnp.concatenate(sent).astype(jnp.bfloat16), rows_here)
        received, names = [], []
        for i, (a, b) in enumerate(steps):
            part = sent[i * room : (i + 1) * room]
            if (a, b) != (0, 0):
                pairs = [(moved(*p), moved(p[0] + a, p[1] + b)) for p in places]
                part = lax.ppermute(part, ("z", "x"), pairs)
            source = moved(own["z"] - a, own["x"] - b)
            comes = (own_owners[source] == member)[None, :] & (own_rank[source][None, :] == seat[:, None])
            received.append(part)
            names.append(jnp.max(jnp.where(comes, own_slots[source][None, :], -1), axis=1))
        out_slots = member * rows + jnp.arange(rows)
        pick = out_slots[:, None] == jnp.concatenate(names)[None, :]
        return pick_rows(pick.astype(jnp.bfloat16), jnp.concatenate(received))

    gram = exchange_rows(0, mine)
    inverse_factor = inverse_factor_of(shift_value, packed, group)
    gram = lax.fori_loop(1, rounds, lambda number, total: total + exchange_rows(number, mine), gram)
    on_pivot = (own_group == pivot_group).astype(jnp.float32)
    out_slots = member * rows + jnp.arange(rows)
    shifted_eye = ((out_slots - rotation) % group)[:, None] == index[None, :]
    gram = gram + shift_value[0] * on_pivot * shifted_eye.astype(jnp.float32)
    return lax.dot_general(
        gram, inverse_factor, (((1,), (1,)), ((), ())), precision=HIGHEST, preferred_element_type=jnp.float32
    )


def solution(mesh):
    samp, par = mesh.shape["samp"], mesh.shape["par"]
    y = samp // 2
    x = y if par % y == 0 else 1
    fine = Mesh(mesh.devices.reshape(y, 2, par // x, x), EVERY)
    placed = (P(EVERY, None), P(EVERY), P(), P())
    return jax.shard_map(on_device, mesh=fine, in_specs=placed, out_specs=P(EVERY, None), check_vma=False)
```

```python
import functools

import jax
import jax.numpy as jnp
from jax import lax
from jax.experimental import pallas as pl
from jax.experimental.pallas import tpu as pltpu
from jax.sharding import Mesh, PartitionSpec as P

SLAB = ("y", "core", "x")
EVERY = ("y", "core", "z", "x")
SHARES = (2, 3, 4, 4, 3)
BLOCK = 128
HIGHEST = lax.Precision.HIGHEST


def invert_block(block):
    size = block.shape[0]
    groups = size // 8
    shape = (8, size)
    work = [block[8 * h : 8 * h + 8, :] for h in range(groups)]
    lane = lax.broadcasted_iota(jnp.int32, shape, 1)
    sub = lax.broadcasted_iota(jnp.int32, shape, 0)

    def column(h, j):
        return jnp.broadcast_to(work[h][:, j : j + 1], shape)

    def total(terms):
        while len(terms) > 1:
            terms = [sum(terms[i + 1 : i + 2], terms[i]) for i in range(0, len(terms), 2)]
        return terms[0]

    for g in range(groups):
        first = 8 * g
        inside = (lane >= first) & (lane < first + 8)
        diagonal = [column(g, first + j) for j in range(8)]
        swept = {(i, j): jnp.broadcast_to(diagonal[j][i : i + 1, :], shape) for i in range(8) for j in range(i + 1)}
        current = jnp.where(inside, (lane - first == sub).astype(jnp.float32), work[g])
        rows = [jnp.broadcast_to(current[i : i + 1, :], shape) for i in range(8)]
        inverse = {}

        def at(k, j):
            return (k, j) if k >= j else (j, k)

        for i in range(8):
            root = lax.rsqrt(swept[i, i])
            reciprocal = root * root
            inverse[i, i] = root
            for j in range(i):
                inverse[i, j] = -swept[i, j] * root
            old = {k: swept[at(k, i)] for k in range(8) if k != i}
            scaled = {k: old[k] * reciprocal for k in old}
            for k in old:
                for j in old:
                    if j <= k:
                        swept[k, j] = swept[k, j] - old[k] * scaled[j]
                swept[at(k, i)] = scaled[k]
            swept[i, i] = -reciprocal
        combined = [total([swept[at(j, i)] * rows[i] for i in range(8)]) for j in range(8)]
        for h in range(g + 1, groups):
            terms = [column(h, first + j) * combined[j] for j in range(8)]
            work[h] = total([jnp.where(inside, 0.0, work[h])] + terms)
        done = None
        for i in range(8):
            row = total([inverse[i, j] * rows[j] for j in range(i + 1)])
            done = row if done is None else jnp.where(sub == i, row, done)
        work[g] = done
    full = jnp.concatenate(work, axis=0)
    row_of = lax.broadcasted_iota(jnp.int32, (size, size), 0)
    column_of = lax.broadcasted_iota(jnp.int32, (size, size), 1)
    return jnp.where(column_of <= row_of, full, 0.0)


def three_parts(values):
    high = values.astype(jnp.bfloat16)
    rest = values - high.astype(jnp.float32)
    middle = rest.astype(jnp.bfloat16)
    low = (rest - middle.astype(jnp.float32)).astype(jnp.bfloat16)
    return high, middle, low


def left_parts(values):
    high, middle, low = three_parts(values)
    return jnp.concatenate([high, high, middle, middle, high, low], axis=1)


def right_parts(values):
    high, middle, low = three_parts(values)
    return jnp.concatenate([high, middle, high, middle, low, high], axis=0)


def unpack(packed_ref, out_ref):
    size = out_ref.shape[0]
    band = packed_ref.shape[1] - size
    count = size // band
    out_ref[...] = jnp.zeros(out_ref.shape, jnp.float32)
    for b in range(count // 2):
        c = count - 1 - b
        out_ref[b * band : (b + 1) * band, b * band :] = packed_ref[b * band : (b + 1) * band, : size - b * band]
        out_ref[c * band : (c + 1) * band, c * band :] = packed_ref[b * band : (b + 1) * band, size - b * band :]


def inverse_factor_kernel(first, last, shift_ref, packed_ref, out_ref, parts_ref):
    size = out_ref.shape[0]
    blocks = size // BLOCK
    if first == 0:
        unpack(packed_ref, out_ref)
    else:
        out_ref[...] = packed_ref[...]
    unit = lax.broadcasted_iota(jnp.int32, (BLOCK, BLOCK), 0) == lax.broadcasted_iota(jnp.int32, (BLOCK, BLOCK), 1)

    def dot(left, right):
        return jnp.dot(left, right, preferred_element_type=jnp.float32)

    def step(j, carry):
        here = pl.ds(pl.multiple_of(j * BLOCK, BLOCK), BLOCK)
        inv = invert_block(out_ref[here, here] + jnp.where(unit, shift_ref[0], 0.0))
        parts_ref[...] = right_parts(out_ref[here, :])
        out_ref[here, :] = dot(left_parts(inv), parts_ref[...])
        out_ref[here, here] = inv
        parts_ref[...] = right_parts(out_ref[here, :])

        def rest(i, carry):
            there = pl.ds(pl.multiple_of(i * BLOCK, BLOCK), BLOCK)
            panel = out_ref[here, there].T
            out_ref[there, here] = jnp.zeros((BLOCK, BLOCK), jnp.float32)
            out_ref[there, :] -= dot(left_parts(panel), parts_ref[...])
            return carry

        return lax.fori_loop(j + 1, blocks, rest, carry)

    lax.fori_loop(first, last, step, 0)
    for j in range(blocks - 1 if last == blocks else 0):
        out_ref[j * BLOCK : (j + 1) * BLOCK, (j + 1) * BLOCK :] = jnp.zeros(
            (BLOCK, size - (j + 1) * BLOCK), jnp.float32
        )


def inverse_factor_of(shift, packed, size, first, last):
    return pl.pallas_call(
        functools.partial(inverse_factor_kernel, first, last),
        out_shape=jax.ShapeDtypeStruct((size, size), jnp.float32),
        in_specs=[pl.BlockSpec(memory_space=pltpu.SMEM), pl.BlockSpec(memory_space=pltpu.VMEM)],
        out_specs=pl.BlockSpec(memory_space=pltpu.VMEM),
        scratch_shapes=[pltpu.VMEM((6 * BLOCK, size), jnp.bfloat16)],
        compiler_params=pltpu.CompilerParams(vmem_limit_bytes=40 * 1024 * 1024),
        cost_estimate=pl.CostEstimate(flops=12 * size**2 * (last - first) * BLOCK, bytes_accessed=8 * size**2, transcendentals=size),
        name="inverse_factor",
    )(shift, packed)


def thirds(values):
    high = lax.reduce_precision(values, 8, 7)
    rest = values - high
    middle = lax.reduce_precision(rest, 8, 7)
    low = rest - middle
    return [part.astype(jnp.bfloat16) for part in (high, middle, low)]


def dot_last(a, b):
    return lax.dot_general(a, b, (((a.ndim - 1,), (b.ndim - 1,)), ((), ())), preferred_element_type=jnp.float32)


def pick_rows(chosen, values):
    return sum(
        jnp.dot(chosen, part, preferred_element_type=jnp.float32) for part in reversed(thirds(values))
    )


def onward(axis, offset):
    count = lax.axis_size(axis)
    return [(i, (i + offset) % count) for i in range(count)]


def gather(values, axis):
    count = lax.axis_size(axis)
    here = lax.axis_index(axis)
    whole = jnp.zeros((count,) + values.shape, values.dtype)
    for offset in range(count):
        part = lax.ppermute(values, axis, onward(axis, offset)) if offset else values
        whole = lax.dynamic_update_index_in_dim(whole, part, (here - offset) % count, 0)
    return whole


def scatter_sum(values, axis):
    count = lax.axis_size(axis)
    here = lax.axis_index(axis)
    rows = values.shape[0] // count
    total = lax.dynamic_slice_in_dim(values, here * rows, rows, 0)
    for offset in range(1, count):
        part = lax.dynamic_slice_in_dim(values, (here + offset) % count * rows, rows, 0)
        total = total + lax.ppermute(part, axis, onward(axis, offset))
    return total


def on_device(jacobian, sample_slot, panel_index, shift_value):
    rows, params = jacobian.shape
    sizes = {axis: lax.axis_size(axis) for axis in EVERY}
    own = {axis: lax.axis_index(axis) for axis in EVERY}
    layers, across = sizes["z"], sizes["x"]
    slab = lax.axis_size(SLAB)
    width = across * rows
    group = layers * width
    members = layers * across
    samples = group * sizes["y"] * sizes["core"]
    pivot_group = panel_index[0] // group
    rotation = panel_index[0] % group
    own_group = lax.axis_index(("y", "core"))
    member = lax.axis_index(("z", "x"))

    tiles, pivots = [], []
    start = 0
    unit = params // sum(SHARES)
    for share in SHARES:
        if tiles:
            here, tiles[-1] = lax.optimization_barrier((jnp.int32(start), tiles[-1]))
            piece = lax.dynamic_slice_in_dim(jacobian, here * unit, share * unit, axis=1)
        else:
            piece = lax.slice_in_dim(jacobian, 0, share * unit, axis=1)
        start += share
        tiles.append(lax.all_to_all(piece, SLAB, split_axis=1, concat_axis=0, tiled=True))
        near = lax.dynamic_slice_in_dim(tiles[-1], pivot_group * width, width, 0)
        pivots.append(lax.all_gather(near, "z", axis=0, tiled=True))

    slots, tiles[-1] = lax.optimization_barrier((sample_slot, tiles[-1]))
    for axis in reversed(EVERY):
        slots = gather(slots, axis)
    slots = slots.reshape(samples // group, group)
    pivot_slots = lax.dynamic_index_in_dim(slots, pivot_group, 0, keepdims=False)
    index = jnp.arange(group)
    pick = (index[:, None] == ((pivot_slots - rotation) % group)[None, :]).astype(jnp.bfloat16)

    band = group // (2 * layers)
    low, high = own["z"] * band, (2 * layers - 1 - own["z"]) * band
    panel = lower = upper = 0.0
    for tile, gathered in zip(tiles, pivots):
        ordered = jnp.dot(pick, gathered, preferred_element_type=jnp.float32).astype(jnp.bfloat16)
        panel = panel + dot_last(tile, ordered)
        lower = lower + dot_last(lax.dynamic_slice_in_dim(ordered, low, band, 0), ordered)
        upper = upper + dot_last(lax.dynamic_slice_in_dim(ordered, high, band, 0), ordered)

    place = jnp.arange(group + band)[None, :]
    lower = lax.dynamic_slice_in_dim(jnp.pad(lower, ((0, 0), (0, group))), low, group + band, 1)
    upper = jnp.pad(upper, ((0, 0), (band, 0)))
    packed = jnp.where(place < group - low, lower, upper) / samples
    summed = scatter_sum(packed, "core")
    cut = summed.shape[0] // 2
    one = scatter_sum(scatter_sum(summed[:cut], "x"), "y")
    two = scatter_sum(scatter_sum(summed[cut:], "y"), "x")
    layered = gather(jnp.concatenate([one, two]), "z")
    few = one.shape[0]
    one = gather(gather(layered[:, :few], "y"), "x")
    two = gather(gather(layered[:, few:], "x"), "y")
    packed = jnp.concatenate([one.reshape(-1, layers, few, group + band), two.reshape(-1, layers, few, group + band)])
    packed = gather(packed, "core")
    packed = packed.transpose(2, 0, 1, 3, 4).reshape(layers * band, group + band)

    mine = lax.psum_scatter(panel / samples, SLAB, scatter_dimension=0, tiled=True)

    room = 8 * -(-5 * rows // 128)
    owners = (slots // rows).reshape(-1, members, rows)
    earlier = jnp.arange(rows)[:, None] > jnp.arange(rows)[None, :]
    alike = owners[..., :, None] == owners[..., None, :]
    rank = jnp.sum(alike & earlier, axis=-1)
    rounds = jnp.max(rank) // room + 1
    own_slots = lax.dynamic_index_in_dim(slots, own_group, 0, keepdims=False).reshape(members, rows)
    own_owners = lax.dynamic_index_in_dim(owners, own_group, 0, keepdims=False)
    own_rank = lax.dynamic_index_in_dim(rank, own_group, 0, keepdims=False)
    targets = jnp.arange(members)
    out_slots = member * rows + jnp.arange(rows)

    def exchange_rows(number, rows_here):
        seat = number * room + jnp.arange(room)
        goes = (own_owners[member][None, None, :] == targets[:, None, None]) & (
            own_rank[member][None, None, :] == seat[None, :, None]
        )
        sent = pick_rows(goes.reshape(members * room, rows).astype(jnp.bfloat16), rows_here)
        received = lax.all_to_all(sent, ("z", "x"), split_axis=0, concat_axis=0, tiled=True)
        comes = (own_owners == member)[:, None, :] & (own_rank[:, None, :] == seat[None, :, None])
        names = jnp.max(jnp.where(comes, own_slots[:, None, :], -1), axis=2).reshape(members * room)
        return pick_rows((out_slots[:, None] == names[None, :]).astype(jnp.bfloat16), received)

    blocks = group // BLOCK
    first = blocks // 4
    begun = inverse_factor_of(shift_value, packed, group, 0, first)
    mine, begun = lax.optimization_barrier((mine, begun))
    gram = exchange_rows(0, mine)
    inverse_factor = inverse_factor_of(shift_value, begun, group, first, blocks)
    gram = lax.fori_loop(1, rounds, lambda number, total: total + exchange_rows(number, mine), gram)
    on_pivot = (own_group == pivot_group).astype(jnp.float32)
    shifted_eye = ((out_slots - rotation) % group)[:, None] == index[None, :]
    gram = gram + shift_value[0] * on_pivot * shifted_eye.astype(jnp.float32)
    return lax.dot_general(
        gram, inverse_factor, (((1,), (1,)), ((), ())), precision=HIGHEST, preferred_element_type=jnp.float32
    )


def solution(mesh):
    samp, par = mesh.shape["samp"], mesh.shape["par"]
    y = samp // 2
    x = y if par % y == 0 else 1
    fine = Mesh(mesh.devices.reshape(y, 2, par // x, x), EVERY)
    placed = (P(EVERY, None), P(EVERY), P(), P())
    return jax.shard_map(on_device, mesh=fine, in_specs=placed, out_specs=P(EVERY, None), check_vma=False)
```

```python
import functools

import jax
import jax.numpy as jnp
from jax import lax
from jax.experimental import pallas as pl
from jax.experimental.layout import Layout, with_layout_constraint
from jax.experimental.pallas import tpu as pltpu
from jax.sharding import Mesh, PartitionSpec as P

SLAB = ("y", "core", "x")
EVERY = ("y", "core", "z", "x")
SHARES = (1, 2, 3, 4, 4, 2)
BLOCK = 128
HIGHEST = lax.Precision.HIGHEST


def invert_block(block):
    size = block.shape[0]
    groups = size // 8
    shape = (8, size)
    work = [block[8 * h : 8 * h + 8, :] for h in range(groups)]
    lane = lax.broadcasted_iota(jnp.int32, shape, 1)
    sub = lax.broadcasted_iota(jnp.int32, shape, 0)

    def column(h, j):
        return jnp.broadcast_to(work[h][:, j : j + 1], shape)

    def total(terms):
        while len(terms) > 1:
            terms = [sum(terms[i + 1 : i + 2], terms[i]) for i in range(0, len(terms), 2)]
        return terms[0]

    for g in range(groups):
        first = 8 * g
        inside = (lane >= first) & (lane < first + 8)
        diagonal = [column(g, first + j) for j in range(8)]
        swept = {(i, j): jnp.broadcast_to(diagonal[j][i : i + 1, :], shape) for i in range(8) for j in range(i + 1)}
        current = jnp.where(inside, (lane - first == sub).astype(jnp.float32), work[g])
        rows = [jnp.broadcast_to(current[i : i + 1, :], shape) for i in range(8)]
        inverse = {}

        def at(k, j):
            return (k, j) if k >= j else (j, k)

        for i in range(8):
            root = lax.rsqrt(swept[i, i])
            reciprocal = root * root
            inverse[i, i] = root
            for j in range(i):
                inverse[i, j] = -swept[i, j] * root
            old = {k: swept[at(k, i)] for k in range(8) if k != i}
            scaled = {k: old[k] * reciprocal for k in old}
            for k in old:
                for j in old:
                    if j <= k:
                        swept[k, j] = swept[k, j] - old[k] * scaled[j]
                swept[at(k, i)] = scaled[k]
            swept[i, i] = -reciprocal
        combined = [total([swept[at(j, i)] * rows[i] for i in range(8)]) for j in range(8)]
        for h in range(g + 1, groups):
            terms = [column(h, first + j) * combined[j] for j in range(8)]
            work[h] = total([jnp.where(inside, 0.0, work[h])] + terms)
        done = None
        for i in range(8):
            row = total([inverse[i, j] * rows[j] for j in range(i + 1)])
            done = row if done is None else jnp.where(sub == i, row, done)
        work[g] = done
    full = jnp.concatenate(work, axis=0)
    row_of = lax.broadcasted_iota(jnp.int32, (size, size), 0)
    column_of = lax.broadcasted_iota(jnp.int32, (size, size), 1)
    return jnp.where(column_of <= row_of, full, 0.0)


def three_parts(values):
    high = values.astype(jnp.bfloat16)
    rest = values - high.astype(jnp.float32)
    middle = rest.astype(jnp.bfloat16)
    low = (rest - middle.astype(jnp.float32)).astype(jnp.bfloat16)
    return high, middle, low


def left_parts(values):
    high, middle, low = three_parts(values)
    return jnp.concatenate([high, high, middle, middle, high, low], axis=1)


def right_parts(values):
    high, middle, low = three_parts(values)
    return jnp.concatenate([high, middle, high, middle, low, high], axis=0)


def unpack(packed_ref, out_ref):
    size = out_ref.shape[0]
    band = packed_ref.shape[1] - size
    count = size // band
    out_ref[...] = jnp.zeros(out_ref.shape, jnp.float32)
    for b in range(count // 2):
        c = count - 1 - b
        out_ref[b * band : (b + 1) * band, b * band :] = packed_ref[b * band : (b + 1) * band, : size - b * band]
        out_ref[c * band : (c + 1) * band, c * band :] = packed_ref[b * band : (b + 1) * band, size - b * band :]


def inverse_factor_kernel(first, last, shift_ref, packed_ref, out_ref, parts_ref):
    size = out_ref.shape[0]
    blocks = size // BLOCK
    if first == 0:
        unpack(packed_ref, out_ref)
    else:
        out_ref[...] = packed_ref[...]
    unit = lax.broadcasted_iota(jnp.int32, (BLOCK, BLOCK), 0) == lax.broadcasted_iota(jnp.int32, (BLOCK, BLOCK), 1)

    def dot(left, right):
        return jnp.dot(left, right, preferred_element_type=jnp.float32)

    def step(j, carry):
        here = pl.ds(pl.multiple_of(j * BLOCK, BLOCK), BLOCK)
        inv = invert_block(out_ref[here, here] + jnp.where(unit, shift_ref[0], 0.0))
        parts_ref[...] = right_parts(out_ref[here, :])
        out_ref[here, :] = dot(left_parts(inv), parts_ref[...])
        out_ref[here, here] = inv
        parts_ref[...] = right_parts(out_ref[here, :])

        def rest(i, carry):
            there = pl.ds(pl.multiple_of(i * BLOCK, BLOCK), BLOCK)
            panel = out_ref[here, there].T
            out_ref[there, here] = jnp.zeros((BLOCK, BLOCK), jnp.float32)
            out_ref[there, :] -= dot(left_parts(panel), parts_ref[...])
            return carry

        return lax.fori_loop(j + 1, blocks, rest, carry)

    lax.fori_loop(first, last, step, 0)
    for j in range(blocks - 1 if last == blocks else 0):
        out_ref[j * BLOCK : (j + 1) * BLOCK, (j + 1) * BLOCK :] = jnp.zeros(
            (BLOCK, size - (j + 1) * BLOCK), jnp.float32
        )


def inverse_factor_of(shift, packed, size, first, last):
    return pl.pallas_call(
        functools.partial(inverse_factor_kernel, first, last),
        out_shape=jax.ShapeDtypeStruct((size, size), jnp.float32),
        in_specs=[pl.BlockSpec(memory_space=pltpu.SMEM), pl.BlockSpec(memory_space=pltpu.VMEM)],
        out_specs=pl.BlockSpec(memory_space=pltpu.VMEM),
        scratch_shapes=[pltpu.VMEM((6 * BLOCK, size), jnp.bfloat16)],
        compiler_params=pltpu.CompilerParams(vmem_limit_bytes=40 * 1024 * 1024),
        cost_estimate=pl.CostEstimate(flops=12 * size**2 * (last - first) * BLOCK, bytes_accessed=8 * size**2, transcendentals=size),
        name="inverse_factor",
    )(shift, packed)


def thirds(values):
    high = lax.reduce_precision(values, 8, 7)
    rest = values - high
    middle = lax.reduce_precision(rest, 8, 7)
    low = rest - middle
    return [part.astype(jnp.bfloat16) for part in (high, middle, low)]


def dot_last(a, b):
    return lax.dot_general(a, b, (((a.ndim - 1,), (b.ndim - 1,)), ((), ())), preferred_element_type=jnp.float32)


def pick_rows(chosen, values):
    return sum(
        jnp.dot(chosen, part, preferred_element_type=jnp.float32) for part in reversed(thirds(values))
    )


def onward(axis, offset):
    count = lax.axis_size(axis)
    return [(i, (i + offset) % count) for i in range(count)]


def gather(values, axis):
    count = lax.axis_size(axis)
    here = lax.axis_index(axis)
    whole = jnp.zeros((count,) + values.shape, values.dtype)
    for offset in range(count):
        part = lax.ppermute(values, axis, onward(axis, offset)) if offset else values
        whole = lax.dynamic_update_index_in_dim(whole, part, (here - offset) % count, 0)
    return whole


def scatter_sum(values, axis):
    count = lax.axis_size(axis)
    here = lax.axis_index(axis)
    rows = values.shape[0] // count
    total = lax.dynamic_slice_in_dim(values, here * rows, rows, 0)
    for offset in range(1, count):
        part = lax.dynamic_slice_in_dim(values, (here + offset) % count * rows, rows, 0)
        total = total + lax.ppermute(part, axis, onward(axis, offset))
    return total


def on_device(jacobian, sample_slot, panel_index, shift_value):
    rows, params = jacobian.shape
    sizes = {axis: lax.axis_size(axis) for axis in EVERY}
    own = {axis: lax.axis_index(axis) for axis in EVERY}
    layers, across = sizes["z"], sizes["x"]
    slab = lax.axis_size(SLAB)
    width = across * rows
    group = layers * width
    members = layers * across
    samples = group * sizes["y"] * sizes["core"]
    pivot_group = panel_index[0] // group
    rotation = panel_index[0] % group
    own_group = lax.axis_index(("y", "core"))
    member = lax.axis_index(("z", "x"))

    tiles, pivots, rings, moved = [], [], [], []
    start = 0
    unit = params // slab // sum(SHARES)
    eights = rows // 8
    strips = with_layout_constraint(jacobian.reshape(eights, 8, slab, params // slab), Layout((0, 2, 1, 3)))
    for share in SHARES:
        if tiles:
            here, tiles[-1], *moved = lax.optimization_barrier((jnp.int32(start), tiles[-1], *moved))
            for ring, piece in zip(moving, moved):
                ring.append(piece)
            piece = lax.dynamic_slice_in_dim(strips, here * unit, share * unit, axis=3)
        else:
            piece = lax.slice_in_dim(strips, 0, share * unit, axis=3)
        start += share
        moving = [ring for ring in rings if len(ring) < layers]
        moved = [lax.ppermute(ring[-1], "z", onward("z", 1)) for ring in moving]
        piece = with_layout_constraint(piece.transpose(2, 0, 1, 3), Layout((0, 1, 2, 3))).reshape(slab, rows, -1)
        tile = lax.all_to_all(piece, SLAB, split_axis=0, concat_axis=0, tiled=True)
        tile = with_layout_constraint(tile, Layout((0, 1, 2))).reshape(slab * rows, -1)
        near = lax.dynamic_slice_in_dim(tile, pivot_group * width, width, 0)
        cut = near.shape[1] * 3 // 4
        tiles.append(tile)
        pivots.append(lax.all_gather(near[:, :cut], "z", axis=0, tiled=True))
        rings.append([near[:, cut:]])
    for ring, piece in zip(moving, moved):
        ring.append(piece)
    for _ in range(layers):
        for ring in rings:
            if len(ring) < layers:
                ring.append(lax.ppermute(ring[-1], "z", onward("z", 1)))

    slots, tiles[-1] = lax.optimization_barrier((sample_slot, tiles[-1]))
    for axis in reversed(EVERY):
        slots = gather(slots, axis)
    slots = slots.reshape(samples // group, group)
    pivot_slots = lax.dynamic_index_in_dim(slots, pivot_group, 0, keepdims=False)
    index = jnp.arange(group)
    pick = (index[:, None] == ((pivot_slots - rotation) % group)[None, :]).astype(jnp.bfloat16)

    band = group // (2 * layers)
    low, high = own["z"] * band, (2 * layers - 1 - own["z"]) * band
    panel = lower = upper = 0.0
    for chunk, (tile, gathered, ring) in enumerate(zip(tiles, pivots, rings)):
        passed = jnp.zeros((group, ring[0].shape[1]), ring[0].dtype)
        for r, piece in enumerate(ring):
            passed = lax.dynamic_update_slice_in_dim(passed, piece, (own["z"] - r) % layers * width, 0)
        gathered = jnp.concatenate([gathered, passed], axis=1)
        ordered = jnp.dot(pick, gathered, preferred_element_type=jnp.float32).astype(jnp.bfloat16)
        panel = panel + dot_last(tile, ordered)
        lower = lower + dot_last(lax.dynamic_slice_in_dim(ordered, low, band, 0), ordered)
        upper = upper + dot_last(lax.dynamic_slice_in_dim(ordered, high, band, 0), ordered)
        if chunk + 1 < len(tiles):
            panel, lower, upper = lax.optimization_barrier((panel, lower, upper))

    place = jnp.arange(group + band)[None, :]
    lower = lax.dynamic_slice_in_dim(jnp.pad(lower, ((0, 0), (0, group))), low, group + band, 1)
    upper = jnp.pad(upper, ((0, 0), (band, 0)))
    packed = jnp.where(place < group - low, lower, upper) / samples
    summed = scatter_sum(packed, "core")
    cut = summed.shape[0] // 2
    one = scatter_sum(scatter_sum(summed[:cut], "x"), "y")
    two = scatter_sum(scatter_sum(summed[cut:], "y"), "x")
    layered = gather(jnp.concatenate([one, two]), "z")
    few = one.shape[0]
    one = gather(gather(layered[:, :few], "y"), "x")
    two = gather(gather(layered[:, few:], "x"), "y")
    packed = jnp.concatenate([one.reshape(-1, layers, few, group + band), two.reshape(-1, layers, few, group + band)])
    packed = gather(packed, "core")
    packed = packed.transpose(2, 0, 1, 3, 4).reshape(layers * band, group + band)

    mine = lax.psum_scatter(panel / samples, SLAB, scatter_dimension=0, tiled=True)

    room = 8 * -(-5 * rows // 128)
    owners = (slots // rows).reshape(-1, members, rows)
    earlier = jnp.arange(rows)[:, None] > jnp.arange(rows)[None, :]
    alike = owners[..., :, None] == owners[..., None, :]
    rank = jnp.sum(alike & earlier, axis=-1)
    rounds = jnp.max(rank) // room + 1
    own_slots = lax.dynamic_index_in_dim(slots, own_group, 0, keepdims=False).reshape(members, rows)
    own_owners = lax.dynamic_index_in_dim(owners, own_group, 0, keepdims=False)
    own_rank = lax.dynamic_index_in_dim(rank, own_group, 0, keepdims=False)
    targets = jnp.arange(members)
    out_slots = member * rows + jnp.arange(rows)

    def exchange_rows(number, rows_here):
        seat = number * room + jnp.arange(room)
        goes = (own_owners[member][None, None, :] == targets[:, None, None]) & (
            own_rank[member][None, None, :] == seat[None, :, None]
        )
        sent = pick_rows(goes.reshape(members * room, rows).astype(jnp.bfloat16), rows_here)
        received = lax.all_to_all(sent, ("z", "x"), split_axis=0, concat_axis=0, tiled=True)
        comes = (own_owners == member)[:, None, :] & (own_rank[:, None, :] == seat[None, :, None])
        names = jnp.max(jnp.where(comes, own_slots[:, None, :], -1), axis=2).reshape(members * room)
        return pick_rows((out_slots[:, None] == names[None, :]).astype(jnp.bfloat16), received)

    blocks = group // BLOCK
    first = blocks // 4
    begun = inverse_factor_of(shift_value, packed, group, 0, first)
    mine, begun = lax.optimization_barrier((mine, begun))
    gram = exchange_rows(0, mine)
    inverse_factor = inverse_factor_of(shift_value, begun, group, first, blocks)
    gram = lax.fori_loop(1, rounds, lambda number, total: total + exchange_rows(number, mine), gram)
    on_pivot = (own_group == pivot_group).astype(jnp.float32)
    shifted_eye = ((out_slots - rotation) % group)[:, None] == index[None, :]
    gram = gram + shift_value[0] * on_pivot * shifted_eye.astype(jnp.float32)
    return lax.dot_general(
        gram, inverse_factor, (((1,), (1,)), ((), ())), precision=HIGHEST, preferred_element_type=jnp.float32
    )


def solution(mesh):
    samp, par = mesh.shape["samp"], mesh.shape["par"]
    y = samp // 2
    x = y if par % y == 0 else 1
    fine = Mesh(mesh.devices.reshape(y, 2, par // x, x), EVERY)
    placed = (P(EVERY, None), P(EVERY), P(), P())
    return jax.shard_map(on_device, mesh=fine, in_specs=placed, out_specs=P(EVERY, None), check_vma=False)
```

```python
import functools

import jax
import jax.numpy as jnp
from jax import lax
from jax.experimental import pallas as pl
from jax.experimental.layout import Layout, with_layout_constraint
from jax.experimental.pallas import tpu as pltpu
from jax.sharding import Mesh, PartitionSpec as P

SLAB = ("y", "core", "x")
EVERY = ("y", "core", "z", "x")
SHARES = (2, 3, 4, 5, 2)
BLOCK = 128
HIGHEST = lax.Precision.HIGHEST


def invert_block(block):
    size = block.shape[0]
    groups = size // 8
    shape = (8, size)
    work = [block[8 * h : 8 * h + 8, :] for h in range(groups)]
    lane = lax.broadcasted_iota(jnp.int32, shape, 1)
    sub = lax.broadcasted_iota(jnp.int32, shape, 0)

    def column(h, j):
        return jnp.broadcast_to(work[h][:, j : j + 1], shape)

    def total(terms):
        while len(terms) > 1:
            terms = [sum(terms[i + 1 : i + 2], terms[i]) for i in range(0, len(terms), 2)]
        return terms[0]

    for g in range(groups):
        first = 8 * g
        inside = (lane >= first) & (lane < first + 8)
        diagonal = [column(g, first + j) for j in range(8)]
        swept = {(i, j): jnp.broadcast_to(diagonal[j][i : i + 1, :], shape) for i in range(8) for j in range(i + 1)}
        current = jnp.where(inside, (lane - first == sub).astype(jnp.float32), work[g])
        rows = [jnp.broadcast_to(current[i : i + 1, :], shape) for i in range(8)]
        inverse = {}

        def at(k, j):
            return (k, j) if k >= j else (j, k)

        for i in range(8):
            root = lax.rsqrt(swept[i, i])
            reciprocal = root * root
            inverse[i, i] = root
            for j in range(i):
                inverse[i, j] = -swept[i, j] * root
            old = {k: swept[at(k, i)] for k in range(8) if k != i}
            scaled = {k: old[k] * reciprocal for k in old}
            for k in old:
                for j in old:
                    if j <= k:
                        swept[k, j] = swept[k, j] - old[k] * scaled[j]
                swept[at(k, i)] = scaled[k]
            swept[i, i] = -reciprocal
        combined = [total([swept[at(j, i)] * rows[i] for i in range(8)]) for j in range(8)]
        for h in range(g + 1, groups):
            terms = [column(h, first + j) * combined[j] for j in range(8)]
            work[h] = total([jnp.where(inside, 0.0, work[h])] + terms)
        done = None
        for i in range(8):
            row = total([inverse[i, j] * rows[j] for j in range(i + 1)])
            done = row if done is None else jnp.where(sub == i, row, done)
        work[g] = done
    full = jnp.concatenate(work, axis=0)
    row_of = lax.broadcasted_iota(jnp.int32, (size, size), 0)
    column_of = lax.broadcasted_iota(jnp.int32, (size, size), 1)
    return jnp.where(column_of <= row_of, full, 0.0)


def three_parts(values):
    high = values.astype(jnp.bfloat16)
    rest = values - high.astype(jnp.float32)
    middle = rest.astype(jnp.bfloat16)
    low = (rest - middle.astype(jnp.float32)).astype(jnp.bfloat16)
    return high, middle, low


def left_parts(values):
    high, middle, low = three_parts(values)
    return jnp.concatenate([high, high, middle, middle, high, low], axis=1)


def right_parts(values):
    high, middle, low = three_parts(values)
    return jnp.concatenate([high, middle, high, middle, low, high], axis=0)


def unpack(packed_ref, out_ref):
    size = out_ref.shape[0]
    band = packed_ref.shape[1] - size
    count = size // band
    out_ref[...] = jnp.zeros(out_ref.shape, jnp.float32)
    for b in range(count // 2):
        c = count - 1 - b
        out_ref[b * band : (b + 1) * band, b * band :] = packed_ref[b * band : (b + 1) * band, : size - b * band]
        out_ref[c * band : (c + 1) * band, c * band :] = packed_ref[b * band : (b + 1) * band, size - b * band :]


def inverse_factor_kernel(first, last, shift_ref, packed_ref, out_ref, parts_ref):
    size = out_ref.shape[0]
    blocks = size // BLOCK
    if first == 0:
        unpack(packed_ref, out_ref)
    else:
        out_ref[...] = packed_ref[...]
    unit = lax.broadcasted_iota(jnp.int32, (BLOCK, BLOCK), 0) == lax.broadcasted_iota(jnp.int32, (BLOCK, BLOCK), 1)

    def dot(left, right):
        return jnp.dot(left, right, preferred_element_type=jnp.float32)

    def step(j, carry):
        here = pl.ds(pl.multiple_of(j * BLOCK, BLOCK), BLOCK)
        inv = invert_block(out_ref[here, here] + jnp.where(unit, shift_ref[0], 0.0))
        parts_ref[...] = right_parts(out_ref[here, :])
        out_ref[here, :] = dot(left_parts(inv), parts_ref[...])
        out_ref[here, here] = inv
        parts_ref[...] = right_parts(out_ref[here, :])

        def rest(i, carry):
            there = pl.ds(pl.multiple_of(i * BLOCK, BLOCK), BLOCK)
            panel = out_ref[here, there].T
            out_ref[there, here] = jnp.zeros((BLOCK, BLOCK), jnp.float32)
            out_ref[there, :] -= dot(left_parts(panel), parts_ref[...])
            return carry

        return lax.fori_loop(j + 1, blocks, rest, carry)

    lax.fori_loop(first, last, step, 0)
    for j in range(blocks - 1 if last == blocks else 0):
        out_ref[j * BLOCK : (j + 1) * BLOCK, (j + 1) * BLOCK :] = jnp.zeros(
            (BLOCK, size - (j + 1) * BLOCK), jnp.float32
        )


def inverse_factor_of(shift, packed, size, first, last):
    return pl.pallas_call(
        functools.partial(inverse_factor_kernel, first, last),
        out_shape=jax.ShapeDtypeStruct((size, size), jnp.float32),
        in_specs=[pl.BlockSpec(memory_space=pltpu.SMEM), pl.BlockSpec(memory_space=pltpu.VMEM)],
        out_specs=pl.BlockSpec(memory_space=pltpu.VMEM),
        scratch_shapes=[pltpu.VMEM((6 * BLOCK, size), jnp.bfloat16)],
        compiler_params=pltpu.CompilerParams(vmem_limit_bytes=40 * 1024 * 1024),
        cost_estimate=pl.CostEstimate(flops=12 * size**2 * (last - first) * BLOCK, bytes_accessed=8 * size**2, transcendentals=size),
        name="inverse_factor",
    )(shift, packed)


def thirds(values):
    high = lax.reduce_precision(values, 8, 7)
    rest = values - high
    middle = lax.reduce_precision(rest, 8, 7)
    low = rest - middle
    return [part.astype(jnp.bfloat16) for part in (high, middle, low)]


def dot_last(a, b):
    return lax.dot_general(a, b, (((a.ndim - 1,), (b.ndim - 1,)), ((), ())), preferred_element_type=jnp.float32)


def pick_rows(chosen, values):
    return sum(
        jnp.dot(chosen, part, preferred_element_type=jnp.float32) for part in reversed(thirds(values))
    )


def onward(axis, offset):
    count = lax.axis_size(axis)
    return [(i, (i + offset) % count) for i in range(count)]


def gather(values, axis):
    count = lax.axis_size(axis)
    here = lax.axis_index(axis)
    whole = jnp.zeros((count,) + values.shape, values.dtype)
    for offset in range(count):
        part = lax.ppermute(values, axis, onward(axis, offset)) if offset else values
        whole = lax.dynamic_update_index_in_dim(whole, part, (here - offset) % count, 0)
    return whole


def scatter_sum(values, axis):
    count = lax.axis_size(axis)
    here = lax.axis_index(axis)
    rows = values.shape[0] // count
    total = lax.dynamic_slice_in_dim(values, here * rows, rows, 0)
    for offset in range(1, count):
        part = lax.dynamic_slice_in_dim(values, (here + offset) % count * rows, rows, 0)
        total = total + lax.ppermute(part, axis, onward(axis, offset))
    return total


def on_device(jacobian, sample_slot, panel_index, shift_value):
    rows, params = jacobian.shape
    sizes = {axis: lax.axis_size(axis) for axis in EVERY}
    own = {axis: lax.axis_index(axis) for axis in EVERY}
    layers, across = sizes["z"], sizes["x"]
    slab = lax.axis_size(SLAB)
    width = across * rows
    group = layers * width
    members = layers * across
    samples = group * sizes["y"] * sizes["core"]
    pivot_group = panel_index[0] // group
    rotation = panel_index[0] % group
    own_group = lax.axis_index(("y", "core"))
    member = lax.axis_index(("z", "x"))

    tiles, pivots = [], []
    start = 0
    unit = params // slab // sum(SHARES)
    eights = rows // 8
    strips = with_layout_constraint(jacobian.reshape(eights, 8, slab, params // slab), Layout((0, 2, 1, 3)))
    for share in SHARES:
        if tiles:
            here, tiles[-1] = lax.optimization_barrier((jnp.int32(start), tiles[-1]))
            piece = lax.dynamic_slice_in_dim(strips, here * unit, share * unit, axis=3)
        else:
            piece = lax.slice_in_dim(strips, 0, share * unit, axis=3)
        start += share
        piece = with_layout_constraint(piece.transpose(2, 0, 1, 3), Layout((0, 1, 2, 3))).reshape(slab, rows, -1)
        tile = lax.all_to_all(piece, SLAB, split_axis=0, concat_axis=0, tiled=True)
        tile = with_layout_constraint(tile, Layout((0, 1, 2))).reshape(slab * rows, -1)
        near = lax.dynamic_slice_in_dim(tile, pivot_group * width, width, 0)
        tiles.append(tile)
        pivots.append(lax.all_gather(near, "z", axis=0, tiled=True))

    slots, tiles[-1] = lax.optimization_barrier((sample_slot, tiles[-1]))
    for axis in reversed(EVERY):
        slots = gather(slots, axis)
    slots = slots.reshape(samples // group, group)
    pivot_slots = lax.dynamic_index_in_dim(slots, pivot_group, 0, keepdims=False)
    index = jnp.arange(group)
    pick = (index[:, None] == ((pivot_slots - rotation) % group)[None, :]).astype(jnp.bfloat16)

    band = group // (2 * layers)
    low, high = own["z"] * band, (2 * layers - 1 - own["z"]) * band
    panel = lower = upper = 0.0
    for chunk, (tile, gathered) in enumerate(zip(tiles, pivots)):
        ordered = jnp.dot(pick, gathered, preferred_element_type=jnp.float32).astype(jnp.bfloat16)
        panel = panel + dot_last(tile, ordered)
        lower = lower + dot_last(lax.dynamic_slice_in_dim(ordered, low, band, 0), ordered)
        upper = upper + dot_last(lax.dynamic_slice_in_dim(ordered, high, band, 0), ordered)
        if chunk + 1 < len(tiles):
            panel, lower, upper = lax.optimization_barrier((panel, lower, upper))

    place = jnp.arange(group + band)[None, :]
    lower = lax.dynamic_slice_in_dim(jnp.pad(lower, ((0, 0), (0, group))), low, group + band, 1)
    upper = jnp.pad(upper, ((0, 0), (band, 0)))
    packed = jnp.where(place < group - low, lower, upper) / samples
    summed = scatter_sum(packed, "core")
    cut = summed.shape[0] // 2
    one = scatter_sum(scatter_sum(summed[:cut], "x"), "y")
    two = scatter_sum(scatter_sum(summed[cut:], "y"), "x")
    layered = gather(jnp.concatenate([one, two]), "z")
    few = one.shape[0]
    one = gather(gather(layered[:, :few], "y"), "x")
    two = gather(gather(layered[:, few:], "x"), "y")
    packed = jnp.concatenate([one.reshape(-1, layers, few, group + band), two.reshape(-1, layers, few, group + band)])
    packed = gather(packed, "core")
    packed = packed.transpose(2, 0, 1, 3, 4).reshape(layers * band, group + band)

    mine = lax.psum_scatter(panel / samples, SLAB, scatter_dimension=0, tiled=True)

    room = 8 * -(-5 * rows // 128)
    owners = (slots // rows).reshape(-1, members, rows)
    earlier = jnp.arange(rows)[:, None] > jnp.arange(rows)[None, :]
    alike = owners[..., :, None] == owners[..., None, :]
    rank = jnp.sum(alike & earlier, axis=-1)
    rounds = jnp.max(rank) // room + 1
    own_slots = lax.dynamic_index_in_dim(slots, own_group, 0, keepdims=False).reshape(members, rows)
    own_owners = lax.dynamic_index_in_dim(owners, own_group, 0, keepdims=False)
    own_rank = lax.dynamic_index_in_dim(rank, own_group, 0, keepdims=False)
    targets = jnp.arange(members)
    out_slots = member * rows + jnp.arange(rows)

    def exchange_rows(number, rows_here):
        seat = number * room + jnp.arange(room)
        goes = (own_owners[member][None, None, :] == targets[:, None, None]) & (
            own_rank[member][None, None, :] == seat[None, :, None]
        )
        sent = pick_rows(goes.reshape(members * room, rows).astype(jnp.bfloat16), rows_here)
        received = lax.all_to_all(sent, ("z", "x"), split_axis=0, concat_axis=0, tiled=True)
        comes = (own_owners == member)[:, None, :] & (own_rank[:, None, :] == seat[None, :, None])
        names = jnp.max(jnp.where(comes, own_slots[:, None, :], -1), axis=2).reshape(members * room)
        return pick_rows((out_slots[:, None] == names[None, :]).astype(jnp.bfloat16), received)

    blocks = group // BLOCK
    first = blocks // 4
    begun = inverse_factor_of(shift_value, packed, group, 0, first)
    mine, begun = lax.optimization_barrier((mine, begun))
    gram = exchange_rows(0, mine)
    inverse_factor = inverse_factor_of(shift_value, begun, group, first, blocks)
    gram = lax.fori_loop(1, rounds, lambda number, total: total + exchange_rows(number, mine), gram)
    on_pivot = (own_group == pivot_group).astype(jnp.float32)
    shifted_eye = ((out_slots - rotation) % group)[:, None] == index[None, :]
    gram = gram + shift_value[0] * on_pivot * shifted_eye.astype(jnp.float32)
    return lax.dot_general(
        gram, inverse_factor, (((1,), (1,)), ((), ())), precision=HIGHEST, preferred_element_type=jnp.float32
    )


def solution(mesh):
    samp, par = mesh.shape["samp"], mesh.shape["par"]
    y = samp // 2
    x = y if par % y == 0 else 1
    fine = Mesh(mesh.devices.reshape(y, 2, par // x, x), EVERY)
    placed = (P(EVERY, None), P(EVERY), P(), P())
    return jax.shard_map(on_device, mesh=fine, in_specs=placed, out_specs=P(EVERY, None), check_vma=False)
```

```python
import functools

import jax
import jax.numpy as jnp
from jax import lax
from jax.experimental import pallas as pl
from jax.experimental.layout import Layout, with_layout_constraint
from jax.experimental.pallas import tpu as pltpu
from jax.sharding import Mesh, PartitionSpec as P

SLAB = ("y", "core", "x")
EVERY = ("y", "core", "z", "x")
SHARES = (2, 3, 4, 4, 3)
PASSED = 3
BLOCK = 128
HIGHEST = lax.Precision.HIGHEST


def invert_block(block):
    size = block.shape[0]
    groups = size // 8
    shape = (8, size)
    work = [block[8 * h : 8 * h + 8, :] for h in range(groups)]
    lane = lax.broadcasted_iota(jnp.int32, shape, 1)
    sub = lax.broadcasted_iota(jnp.int32, shape, 0)

    def column(h, j):
        return jnp.broadcast_to(work[h][:, j : j + 1], shape)

    def total(terms):
        while len(terms) > 1:
            terms = [sum(terms[i + 1 : i + 2], terms[i]) for i in range(0, len(terms), 2)]
        return terms[0]

    for g in range(groups):
        first = 8 * g
        inside = (lane >= first) & (lane < first + 8)
        diagonal = [column(g, first + j) for j in range(8)]
        swept = {(i, j): jnp.broadcast_to(diagonal[j][i : i + 1, :], shape) for i in range(8) for j in range(i + 1)}
        current = jnp.where(inside, (lane - first == sub).astype(jnp.float32), work[g])
        rows = [jnp.broadcast_to(current[i : i + 1, :], shape) for i in range(8)]
        inverse = {}

        def at(k, j):
            return (k, j) if k >= j else (j, k)

        for i in range(8):
            root = lax.rsqrt(swept[i, i])
            reciprocal = root * root
            inverse[i, i] = root
            for j in range(i):
                inverse[i, j] = -swept[i, j] * root
            old = {k: swept[at(k, i)] for k in range(8) if k != i}
            scaled = {k: old[k] * reciprocal for k in old}
            for k in old:
                for j in old:
                    if j <= k:
                        swept[k, j] = swept[k, j] - old[k] * scaled[j]
                swept[at(k, i)] = scaled[k]
            swept[i, i] = -reciprocal
        combined = [total([swept[at(j, i)] * rows[i] for i in range(8)]) for j in range(8)]
        for h in range(g + 1, groups):
            terms = [column(h, first + j) * combined[j] for j in range(8)]
            work[h] = total([jnp.where(inside, 0.0, work[h])] + terms)
        done = None
        for i in range(8):
            row = total([inverse[i, j] * rows[j] for j in range(i + 1)])
            done = row if done is None else jnp.where(sub == i, row, done)
        work[g] = done
    full = jnp.concatenate(work, axis=0)
    row_of = lax.broadcasted_iota(jnp.int32, (size, size), 0)
    column_of = lax.broadcasted_iota(jnp.int32, (size, size), 1)
    return jnp.where(column_of <= row_of, full, 0.0)


def three_parts(values):
    high = values.astype(jnp.bfloat16)
    rest = values - high.astype(jnp.float32)
    middle = rest.astype(jnp.bfloat16)
    low = (rest - middle.astype(jnp.float32)).astype(jnp.bfloat16)
    return high, middle, low


def left_parts(values):
    high, middle, low = three_parts(values)
    return jnp.concatenate([high, high, middle, middle, high, low], axis=1)


def right_parts(values):
    high, middle, low = three_parts(values)
    return jnp.concatenate([high, middle, high, middle, low, high], axis=0)


def unpack(packed_ref, out_ref):
    size = out_ref.shape[0]
    band = packed_ref.shape[1] - size
    count = size // band
    out_ref[...] = jnp.zeros(out_ref.shape, jnp.float32)
    for b in range(count // 2):
        c = count - 1 - b
        out_ref[b * band : (b + 1) * band, b * band :] = packed_ref[b * band : (b + 1) * band, : size - b * band]
        out_ref[c * band : (c + 1) * band, c * band :] = packed_ref[b * band : (b + 1) * band, size - b * band :]


def inverse_factor_kernel(first, last, shift_ref, packed_ref, out_ref, parts_ref):
    size = out_ref.shape[0]
    blocks = size // BLOCK
    if first == 0:
        unpack(packed_ref, out_ref)
    else:
        out_ref[...] = packed_ref[...]
    unit = lax.broadcasted_iota(jnp.int32, (BLOCK, BLOCK), 0) == lax.broadcasted_iota(jnp.int32, (BLOCK, BLOCK), 1)

    def dot(left, right):
        return jnp.dot(left, right, preferred_element_type=jnp.float32)

    def step(j, carry):
        here = pl.ds(pl.multiple_of(j * BLOCK, BLOCK), BLOCK)
        inv = invert_block(out_ref[here, here] + jnp.where(unit, shift_ref[0], 0.0))
        parts_ref[...] = right_parts(out_ref[here, :])
        out_ref[here, :] = dot(left_parts(inv), parts_ref[...])
        out_ref[here, here] = inv
        parts_ref[...] = right_parts(out_ref[here, :])

        def rest(i, carry):
            there = pl.ds(pl.multiple_of(i * BLOCK, BLOCK), BLOCK)
            panel = out_ref[here, there].T
            out_ref[there, here] = jnp.zeros((BLOCK, BLOCK), jnp.float32)
            out_ref[there, :] -= dot(left_parts(panel), parts_ref[...])
            return carry

        return lax.fori_loop(j + 1, blocks, rest, carry)

    lax.fori_loop(first, last, step, 0)
    for j in range(blocks - 1 if last == blocks else 0):
        out_ref[j * BLOCK : (j + 1) * BLOCK, (j + 1) * BLOCK :] = jnp.zeros(
            (BLOCK, size - (j + 1) * BLOCK), jnp.float32
        )


def inverse_factor_of(shift, packed, size, first, last):
    return pl.pallas_call(
        functools.partial(inverse_factor_kernel, first, last),
        out_shape=jax.ShapeDtypeStruct((size, size), jnp.float32),
        in_specs=[pl.BlockSpec(memory_space=pltpu.SMEM), pl.BlockSpec(memory_space=pltpu.VMEM)],
        out_specs=pl.BlockSpec(memory_space=pltpu.VMEM),
        scratch_shapes=[pltpu.VMEM((6 * BLOCK, size), jnp.bfloat16)],
        compiler_params=pltpu.CompilerParams(vmem_limit_bytes=40 * 1024 * 1024),
        cost_estimate=pl.CostEstimate(flops=12 * size**2 * (last - first) * BLOCK, bytes_accessed=8 * size**2, transcendentals=size),
        name="inverse_factor",
    )(shift, packed)


def thirds(values):
    high = lax.reduce_precision(values, 8, 7)
    rest = values - high
    middle = lax.reduce_precision(rest, 8, 7)
    low = rest - middle
    return [part.astype(jnp.bfloat16) for part in (high, middle, low)]


def dot_last(a, b):
    return lax.dot_general(a, b, (((a.ndim - 1,), (b.ndim - 1,)), ((), ())), preferred_element_type=jnp.float32)


def pick_rows(chosen, values):
    return sum(
        jnp.dot(chosen, part, preferred_element_type=jnp.float32) for part in reversed(thirds(values))
    )


def onward(axis, offset):
    count = lax.axis_size(axis)
    return [(i, (i + offset) % count) for i in range(count)]


def gather(values, axis):
    count = lax.axis_size(axis)
    here = lax.axis_index(axis)
    whole = jnp.zeros((count,) + values.shape, values.dtype)
    for offset in range(count):
        part = lax.ppermute(values, axis, onward(axis, offset)) if offset else values
        whole = lax.dynamic_update_index_in_dim(whole, part, (here - offset) % count, 0)
    return whole


def scatter_sum(values, axis):
    count = lax.axis_size(axis)
    here = lax.axis_index(axis)
    rows = values.shape[0] // count
    total = lax.dynamic_slice_in_dim(values, here * rows, rows, 0)
    for offset in range(1, count):
        part = lax.dynamic_slice_in_dim(values, (here + offset) % count * rows, rows, 0)
        total = total + lax.ppermute(part, axis, onward(axis, offset))
    return total


def on_device(jacobian, sample_slot, panel_index, shift_value):
    rows, params = jacobian.shape
    sizes = {axis: lax.axis_size(axis) for axis in EVERY}
    own = {axis: lax.axis_index(axis) for axis in EVERY}
    layers, across = sizes["z"], sizes["x"]
    slab = lax.axis_size(SLAB)
    width = across * rows
    group = layers * width
    members = layers * across
    samples = group * sizes["y"] * sizes["core"]
    pivot_group = panel_index[0] // group
    rotation = panel_index[0] % group
    own_group = lax.axis_index(("y", "core"))
    member = lax.axis_index(("z", "x"))

    tiles, pivots = [], []
    start = 0
    unit = params // slab // sum(SHARES)
    eights = rows // 8
    strips = with_layout_constraint(jacobian.reshape(eights, 8, slab, params // slab), Layout((0, 2, 1, 3)))
    for chunk, share in enumerate(SHARES):
        if tiles:
            here, tiles[-1] = lax.optimization_barrier((jnp.int32(start), tiles[-1]))
            piece = lax.dynamic_slice_in_dim(strips, here * unit, share * unit, axis=3)
        else:
            piece = lax.slice_in_dim(strips, 0, share * unit, axis=3)
        start += share
        piece = with_layout_constraint(piece.transpose(2, 0, 1, 3), Layout((0, 1, 2, 3))).reshape(slab, rows, -1)
        tile = lax.all_to_all(piece, SLAB, split_axis=0, concat_axis=0, tiled=True)
        tile = with_layout_constraint(tile, Layout((0, 1, 2))).reshape(slab * rows, -1)
        near = lax.dynamic_slice_in_dim(tile, pivot_group * width, width, 0)
        tiles.append(tile)
        if chunk == PASSED:
            ring = [near, lax.ppermute(near, "z", onward("z", 1))]
            pivots.append(None)
        else:
            pivots.append(lax.all_gather(near, "z", axis=0, tiled=True))

    slots, tiles[-1], ring[1] = lax.optimization_barrier((sample_slot, tiles[-1], ring[1]))
    for _ in range(2, layers):
        ring.append(lax.ppermute(ring[-1], "z", onward("z", 1)))
    passed = jnp.zeros((group, ring[0].shape[1]), ring[0].dtype)
    for r, part in enumerate(ring):
        passed = lax.dynamic_update_slice_in_dim(passed, part, (own["z"] - r) % layers * width, 0)
    pivots[PASSED] = passed
    for axis in reversed(EVERY):
        slots = gather(slots, axis)
    slots = slots.reshape(samples // group, group)
    pivot_slots = lax.dynamic_index_in_dim(slots, pivot_group, 0, keepdims=False)
    index = jnp.arange(group)
    pick = (index[:, None] == ((pivot_slots - rotation) % group)[None, :]).astype(jnp.bfloat16)

    band = group // (2 * layers)
    low, high = own["z"] * band, (2 * layers - 1 - own["z"]) * band
    panel = lower = upper = 0.0
    for chunk, (tile, gathered) in enumerate(zip(tiles, pivots)):
        ordered = jnp.dot(pick, gathered, preferred_element_type=jnp.float32).astype(jnp.bfloat16)
        panel = panel + dot_last(tile, ordered)
        lower = lower + dot_last(lax.dynamic_slice_in_dim(ordered, low, band, 0), ordered)
        upper = upper + dot_last(lax.dynamic_slice_in_dim(ordered, high, band, 0), ordered)
        if chunk + 1 < len(tiles):
            panel, lower, upper = lax.optimization_barrier((panel, lower, upper))

    place = jnp.arange(group + band)[None, :]
    lower = lax.dynamic_slice_in_dim(jnp.pad(lower, ((0, 0), (0, group))), low, group + band, 1)
    upper = jnp.pad(upper, ((0, 0), (band, 0)))
    packed = jnp.where(place < group - low, lower, upper) / samples
    summed = scatter_sum(packed, "core")
    cut = summed.shape[0] // 2
    one = scatter_sum(scatter_sum(summed[:cut], "x"), "y")
    two = scatter_sum(scatter_sum(summed[cut:], "y"), "x")
    layered = gather(jnp.concatenate([one, two]), "z")
    few = one.shape[0]
    one = gather(gather(layered[:, :few], "y"), "x")
    two = gather(gather(layered[:, few:], "x"), "y")
    packed = jnp.concatenate([one.reshape(-1, layers, few, group + band), two.reshape(-1, layers, few, group + band)])
    packed = gather(packed, "core")
    packed = packed.transpose(2, 0, 1, 3, 4).reshape(layers * band, group + band)

    mine = lax.psum_scatter(panel / samples, SLAB, scatter_dimension=0, tiled=True)

    room = 8 * -(-5 * rows // 128)
    owners = (slots // rows).reshape(-1, members, rows)
    earlier = jnp.arange(rows)[:, None] > jnp.arange(rows)[None, :]
    alike = owners[..., :, None] == owners[..., None, :]
    rank = jnp.sum(alike & earlier, axis=-1)
    rounds = jnp.max(rank) // room + 1
    own_slots = lax.dynamic_index_in_dim(slots, own_group, 0, keepdims=False).reshape(members, rows)
    own_owners = lax.dynamic_index_in_dim(owners, own_group, 0, keepdims=False)
    own_rank = lax.dynamic_index_in_dim(rank, own_group, 0, keepdims=False)
    targets = jnp.arange(members)
    out_slots = member * rows + jnp.arange(rows)

    def exchange_rows(number, rows_here):
        seat = number * room + jnp.arange(room)
        goes = (own_owners[member][None, None, :] == targets[:, None, None]) & (
            own_rank[member][None, None, :] == seat[None, :, None]
        )
        sent = pick_rows(goes.reshape(members * room, rows).astype(jnp.bfloat16), rows_here)
        received = lax.all_to_all(sent, ("z", "x"), split_axis=0, concat_axis=0, tiled=True)
        comes = (own_owners == member)[:, None, :] & (own_rank[:, None, :] == seat[None, :, None])
        names = jnp.max(jnp.where(comes, own_slots[:, None, :], -1), axis=2).reshape(members * room)
        return pick_rows((out_slots[:, None] == names[None, :]).astype(jnp.bfloat16), received)

    blocks = group // BLOCK
    first = blocks // 4
    begun = inverse_factor_of(shift_value, packed, group, 0, first)
    mine, begun = lax.optimization_barrier((mine, begun))
    gram = exchange_rows(0, mine)
    inverse_factor = inverse_factor_of(shift_value, begun, group, first, blocks)
    gram = lax.fori_loop(1, rounds, lambda number, total: total + exchange_rows(number, mine), gram)
    on_pivot = (own_group == pivot_group).astype(jnp.float32)
    shifted_eye = ((out_slots - rotation) % group)[:, None] == index[None, :]
    gram = gram + shift_value[0] * on_pivot * shifted_eye.astype(jnp.float32)
    return lax.dot_general(
        gram, inverse_factor, (((1,), (1,)), ((), ())), precision=HIGHEST, preferred_element_type=jnp.float32
    )


def solution(mesh):
    samp, par = mesh.shape["samp"], mesh.shape["par"]
    y = samp // 2
    x = y if par % y == 0 else 1
    fine = Mesh(mesh.devices.reshape(y, 2, par // x, x), EVERY)
    placed = (P(EVERY, None), P(EVERY), P(), P())
    return jax.shard_map(on_device, mesh=fine, in_specs=placed, out_specs=P(EVERY, None), check_vma=False)
```

```python
import functools

import jax
import jax.numpy as jnp
from jax import lax
from jax.experimental import pallas as pl
from jax.experimental.layout import Layout, with_layout_constraint
from jax.experimental.pallas import tpu as pltpu
from jax.sharding import Mesh, PartitionSpec as P

SLAB = ("y", "core", "x")
EVERY = ("y", "core", "z", "x")
SHARES = (2, 3, 4, 4, 3)
PASSED = 3
BLOCK = 128
HIGHEST = lax.Precision.HIGHEST


def invert_block(block):
    size = block.shape[0]
    groups = size // 8
    shape = (8, size)
    work = [block[8 * h : 8 * h + 8, :] for h in range(groups)]
    lane = lax.broadcasted_iota(jnp.int32, shape, 1)
    sub = lax.broadcasted_iota(jnp.int32, shape, 0)

    def column(h, j):
        return jnp.broadcast_to(work[h][:, j : j + 1], shape)

    def total(terms):
        while len(terms) > 1:
            terms = [sum(terms[i + 1 : i + 2], terms[i]) for i in range(0, len(terms), 2)]
        return terms[0]

    for g in range(groups):
        first = 8 * g
        inside = (lane >= first) & (lane < first + 8)
        diagonal = [column(g, first + j) for j in range(8)]
        swept = {(i, j): jnp.broadcast_to(diagonal[j][i : i + 1, :], shape) for i in range(8) for j in range(i + 1)}
        current = jnp.where(inside, (lane - first == sub).astype(jnp.float32), work[g])
        rows = [jnp.broadcast_to(current[i : i + 1, :], shape) for i in range(8)]
        inverse = {}

        def at(k, j):
            return (k, j) if k >= j else (j, k)

        for i in range(8):
            root = lax.rsqrt(swept[i, i])
            reciprocal = root * root
            inverse[i, i] = root
            for j in range(i):
                inverse[i, j] = -swept[i, j] * root
            old = {k: swept[at(k, i)] for k in range(8) if k != i}
            scaled = {k: old[k] * reciprocal for k in old}
            for k in old:
                for j in old:
                    if j <= k:
                        swept[k, j] = swept[k, j] - old[k] * scaled[j]
                swept[at(k, i)] = scaled[k]
            swept[i, i] = -reciprocal
        combined = [total([swept[at(j, i)] * rows[i] for i in range(8)]) for j in range(8)]
        for h in range(g + 1, groups):
            terms = [column(h, first + j) * combined[j] for j in range(8)]
            work[h] = total([jnp.where(inside, 0.0, work[h])] + terms)
        done = None
        for i in range(8):
            row = total([inverse[i, j] * rows[j] for j in range(i + 1)])
            done = row if done is None else jnp.where(sub == i, row, done)
        work[g] = done
    full = jnp.concatenate(work, axis=0)
    row_of = lax.broadcasted_iota(jnp.int32, (size, size), 0)
    column_of = lax.broadcasted_iota(jnp.int32, (size, size), 1)
    return jnp.where(column_of <= row_of, full, 0.0)


def three_parts(values):
    high = values.astype(jnp.bfloat16)
    rest = values - high.astype(jnp.float32)
    middle = rest.astype(jnp.bfloat16)
    low = (rest - middle.astype(jnp.float32)).astype(jnp.bfloat16)
    return high, middle, low


def left_parts(values):
    high, middle, low = three_parts(values)
    return jnp.concatenate([high, high, middle, middle, high, low], axis=1)


def right_parts(values):
    high, middle, low = three_parts(values)
    return jnp.concatenate([high, middle, high, middle, low, high], axis=0)


def unpack(packed_ref, out_ref):
    size = out_ref.shape[0]
    band = packed_ref.shape[1] - size
    count = size // band
    out_ref[...] = jnp.zeros(out_ref.shape, jnp.float32)
    for b in range(count // 2):
        c = count - 1 - b
        out_ref[b * band : (b + 1) * band, b * band :] = packed_ref[b * band : (b + 1) * band, : size - b * band]
        out_ref[c * band : (c + 1) * band, c * band :] = packed_ref[b * band : (b + 1) * band, size - b * band :]


def inverse_factor_kernel(first, last, shift_ref, packed_ref, out_ref, parts_ref):
    size = out_ref.shape[0]
    blocks = size // BLOCK
    if first == 0:
        unpack(packed_ref, out_ref)
    else:
        out_ref[...] = packed_ref[...]
    unit = lax.broadcasted_iota(jnp.int32, (BLOCK, BLOCK), 0) == lax.broadcasted_iota(jnp.int32, (BLOCK, BLOCK), 1)

    def dot(left, right):
        return jnp.dot(left, right, preferred_element_type=jnp.float32)

    def step(j, carry):
        here = pl.ds(pl.multiple_of(j * BLOCK, BLOCK), BLOCK)
        inv = invert_block(out_ref[here, here] + jnp.where(unit, shift_ref[0], 0.0))
        parts_ref[...] = right_parts(out_ref[here, :])
        out_ref[here, :] = dot(left_parts(inv), parts_ref[...])
        out_ref[here, here] = inv
        parts_ref[...] = right_parts(out_ref[here, :])

        def rest(i, carry):
            there = pl.ds(pl.multiple_of(i * BLOCK, BLOCK), BLOCK)
            panel = out_ref[here, there].T
            out_ref[there, here] = jnp.zeros((BLOCK, BLOCK), jnp.float32)
            out_ref[there, :] -= dot(left_parts(panel), parts_ref[...])
            return carry

        return lax.fori_loop(j + 1, blocks, rest, carry)

    lax.fori_loop(first, last, step, 0)
    for j in range(blocks - 1 if last == blocks else 0):
        out_ref[j * BLOCK : (j + 1) * BLOCK, (j + 1) * BLOCK :] = jnp.zeros(
            (BLOCK, size - (j + 1) * BLOCK), jnp.float32
        )


def inverse_factor_of(shift, packed, size, first, last):
    return pl.pallas_call(
        functools.partial(inverse_factor_kernel, first, last),
        out_shape=jax.ShapeDtypeStruct((size, size), jnp.float32),
        in_specs=[pl.BlockSpec(memory_space=pltpu.SMEM), pl.BlockSpec(memory_space=pltpu.VMEM)],
        out_specs=pl.BlockSpec(memory_space=pltpu.VMEM),
        scratch_shapes=[pltpu.VMEM((6 * BLOCK, size), jnp.bfloat16)],
        compiler_params=pltpu.CompilerParams(vmem_limit_bytes=40 * 1024 * 1024),
        cost_estimate=pl.CostEstimate(flops=12 * size**2 * (last - first) * BLOCK, bytes_accessed=8 * size**2, transcendentals=size),
        name="inverse_factor",
    )(shift, packed)


def thirds(values):
    high = lax.reduce_precision(values, 8, 7)
    rest = values - high
    middle = lax.reduce_precision(rest, 8, 7)
    low = rest - middle
    return [part.astype(jnp.bfloat16) for part in (high, middle, low)]


def dot_last(a, b):
    return lax.dot_general(a, b, (((a.ndim - 1,), (b.ndim - 1,)), ((), ())), preferred_element_type=jnp.float32)


def pick_rows(chosen, values):
    return sum(
        jnp.dot(chosen, part, preferred_element_type=jnp.float32) for part in reversed(thirds(values))
    )


def onward(axis, offset):
    count = lax.axis_size(axis)
    return [(i, (i + offset) % count) for i in range(count)]


def gather(values, axis):
    count = lax.axis_size(axis)
    here = lax.axis_index(axis)
    whole = jnp.zeros((count,) + values.shape, values.dtype)
    for offset in range(count):
        part = lax.ppermute(values, axis, onward(axis, offset)) if offset else values
        whole = lax.dynamic_update_index_in_dim(whole, part, (here - offset) % count, 0)
    return whole


def scatter_sum(values, axis):
    count = lax.axis_size(axis)
    here = lax.axis_index(axis)
    rows = values.shape[0] // count
    total = lax.dynamic_slice_in_dim(values, here * rows, rows, 0)
    for offset in range(1, count):
        part = lax.dynamic_slice_in_dim(values, (here + offset) % count * rows, rows, 0)
        total = total + lax.ppermute(part, axis, onward(axis, offset))
    return total


def on_device(jacobian, sample_slot, panel_index, shift_value):
    rows, params = jacobian.shape
    sizes = {axis: lax.axis_size(axis) for axis in EVERY}
    own = {axis: lax.axis_index(axis) for axis in EVERY}
    layers, across = sizes["z"], sizes["x"]
    slab = lax.axis_size(SLAB)
    width = across * rows
    group = layers * width
    members = layers * across
    samples = group * sizes["y"] * sizes["core"]
    pivot_group = panel_index[0] // group
    rotation = panel_index[0] % group
    own_group = lax.axis_index(("y", "core"))
    member = lax.axis_index(("z", "x"))

    tiles, pivots = [], []
    slots = sample_slot
    start = 0
    unit = params // slab // sum(SHARES)
    eights = rows // 8
    strips = with_layout_constraint(jacobian.reshape(eights, 8, slab, params // slab), Layout((0, 2, 1, 3)))
    for chunk, share in enumerate(SHARES):
        if tiles:
            here, tiles[-1], slots = lax.optimization_barrier((jnp.int32(start), tiles[-1], slots))
            if chunk == 1:
                for axis in reversed(EVERY):
                    slots = gather(slots, axis)
            piece = lax.dynamic_slice_in_dim(strips, here * unit, share * unit, axis=3)
        else:
            piece = lax.slice_in_dim(strips, 0, share * unit, axis=3)
        start += share
        piece = with_layout_constraint(piece.transpose(2, 0, 1, 3), Layout((0, 1, 2, 3))).reshape(slab, rows, -1)
        tile = lax.all_to_all(piece, SLAB, split_axis=0, concat_axis=0, tiled=True)
        tile = with_layout_constraint(tile, Layout((0, 1, 2))).reshape(slab * rows, -1)
        near = lax.dynamic_slice_in_dim(tile, pivot_group * width, width, 0)
        tiles.append(tile)
        if chunk == PASSED:
            ring = [near, lax.ppermute(near, "z", onward("z", 1))]
            pivots.append(None)
        else:
            pivots.append(lax.all_gather(near, "z", axis=0, tiled=True))

    for _ in range(2, layers):
        ring.append(lax.ppermute(ring[-1], "z", onward("z", 1)))
    passed = jnp.zeros((group, ring[0].shape[1]), ring[0].dtype)
    for r, part in enumerate(ring):
        passed = lax.dynamic_update_slice_in_dim(passed, part, (own["z"] - r) % layers * width, 0)
    pivots[PASSED] = passed
    for r in range(1, min(layers - 1, PASSED)):
        pivots[r], _ = lax.optimization_barrier((pivots[r], ring[r]))
    slots = slots.reshape(samples // group, group)
    pivot_slots = lax.dynamic_index_in_dim(slots, pivot_group, 0, keepdims=False)
    index = jnp.arange(group)
    pick = (index[:, None] == ((pivot_slots - rotation) % group)[None, :]).astype(jnp.bfloat16)

    band = group // (2 * layers)
    low, high = own["z"] * band, (2 * layers - 1 - own["z"]) * band
    panel = lower = upper = 0.0
    for chunk, (tile, gathered) in enumerate(zip(tiles, pivots)):
        ordered = jnp.dot(pick, gathered, preferred_element_type=jnp.float32).astype(jnp.bfloat16)
        panel = panel + dot_last(tile, ordered)
        lower = lower + dot_last(lax.dynamic_slice_in_dim(ordered, low, band, 0), ordered)
        upper = upper + dot_last(lax.dynamic_slice_in_dim(ordered, high, band, 0), ordered)
        if chunk + 1 < len(tiles):
            panel, lower, upper = lax.optimization_barrier((panel, lower, upper))

    place = jnp.arange(group + band)[None, :]
    lower = lax.dynamic_slice_in_dim(jnp.pad(lower, ((0, 0), (0, group))), low, group + band, 1)
    upper = jnp.pad(upper, ((0, 0), (band, 0)))
    packed = jnp.where(place < group - low, lower, upper) / samples
    summed = scatter_sum(packed, "core")
    cut = summed.shape[0] // 2
    one = scatter_sum(scatter_sum(summed[:cut], "x"), "y")
    two = scatter_sum(scatter_sum(summed[cut:], "y"), "x")
    layered = gather(jnp.concatenate([one, two]), "z")
    few = one.shape[0]
    one = gather(gather(layered[:, :few], "y"), "x")
    two = gather(gather(layered[:, few:], "x"), "y")
    packed = jnp.concatenate([one.reshape(-1, layers, few, group + band), two.reshape(-1, layers, few, group + band)])
    packed = gather(packed, "core")
    packed = packed.transpose(2, 0, 1, 3, 4).reshape(layers * band, group + band)

    mine = lax.psum_scatter(panel / samples, SLAB, scatter_dimension=0, tiled=True)

    room = 8 * -(-5 * rows // 128)
    owners = (slots // rows).reshape(-1, members, rows)
    earlier = jnp.arange(rows)[:, None] > jnp.arange(rows)[None, :]
    alike = owners[..., :, None] == owners[..., None, :]
    rank = jnp.sum(alike & earlier, axis=-1)
    rounds = jnp.max(rank) // room + 1
    own_slots = lax.dynamic_index_in_dim(slots, own_group, 0, keepdims=False).reshape(members, rows)
    own_owners = lax.dynamic_index_in_dim(owners, own_group, 0, keepdims=False)
    own_rank = lax.dynamic_index_in_dim(rank, own_group, 0, keepdims=False)
    targets = jnp.arange(members)
    out_slots = member * rows + jnp.arange(rows)

    def exchange_rows(number, rows_here):
        seat = number * room + jnp.arange(room)
        goes = (own_owners[member][None, None, :] == targets[:, None, None]) & (
            own_rank[member][None, None, :] == seat[None, :, None]
        )
        sent = pick_rows(goes.reshape(members * room, rows).astype(jnp.bfloat16), rows_here)
        received = lax.all_to_all(sent, ("z", "x"), split_axis=0, concat_axis=0, tiled=True)
        comes = (own_owners == member)[:, None, :] & (own_rank[:, None, :] == seat[None, :, None])
        names = jnp.max(jnp.where(comes, own_slots[:, None, :], -1), axis=2).reshape(members * room)
        return pick_rows((out_slots[:, None] == names[None, :]).astype(jnp.bfloat16), received)

    blocks = group // BLOCK
    first = blocks // 4
    begun = inverse_factor_of(shift_value, packed, group, 0, first)
    mine, begun = lax.optimization_barrier((mine, begun))
    gram = exchange_rows(0, mine)
    inverse_factor = inverse_factor_of(shift_value, begun, group, first, blocks)
    gram = lax.fori_loop(1, rounds, lambda number, total: total + exchange_rows(number, mine), gram)
    on_pivot = (own_group == pivot_group).astype(jnp.float32)
    shifted_eye = ((out_slots - rotation) % group)[:, None] == index[None, :]
    gram = gram + shift_value[0] * on_pivot * shifted_eye.astype(jnp.float32)
    return lax.dot_general(
        gram, inverse_factor, (((1,), (1,)), ((), ())), precision=HIGHEST, preferred_element_type=jnp.float32
    )


def solution(mesh):
    samp, par = mesh.shape["samp"], mesh.shape["par"]
    y = samp // 2
    x = y if par % y == 0 else 1
    fine = Mesh(mesh.devices.reshape(y, 2, par // x, x), EVERY)
    placed = (P(EVERY, None), P(EVERY), P(), P())
    return jax.shard_map(on_device, mesh=fine, in_specs=placed, out_specs=P(EVERY, None), check_vma=False)
```

```python
import functools

import jax
import jax.numpy as jnp
from jax import lax
from jax.experimental import pallas as pl
from jax.experimental.layout import Layout, with_layout_constraint
from jax.experimental.pallas import tpu as pltpu
from jax.sharding import Mesh, PartitionSpec as P

SLAB = ("y", "core", "x")
EVERY = ("y", "core", "z", "x")
SHARES = (2, 3, 4, 4, 3)
PASSED = 3
BLOCK = 128
HIGHEST = lax.Precision.HIGHEST


def invert_block(block):
    size = block.shape[0]
    groups = size // 8
    shape = (8, size)
    work = [block[8 * h : 8 * h + 8, :] for h in range(groups)]
    lane = lax.broadcasted_iota(jnp.int32, shape, 1)
    sub = lax.broadcasted_iota(jnp.int32, shape, 0)

    def column(h, j):
        return jnp.broadcast_to(work[h][:, j : j + 1], shape)

    def total(terms):
        while len(terms) > 1:
            terms = [sum(terms[i + 1 : i + 2], terms[i]) for i in range(0, len(terms), 2)]
        return terms[0]

    for g in range(groups):
        first = 8 * g
        inside = (lane >= first) & (lane < first + 8)
        diagonal = [column(g, first + j) for j in range(8)]
        swept = {(i, j): jnp.broadcast_to(diagonal[j][i : i + 1, :], shape) for i in range(8) for j in range(i + 1)}
        current = jnp.where(inside, (lane - first == sub).astype(jnp.float32), work[g])
        rows = [jnp.broadcast_to(current[i : i + 1, :], shape) for i in range(8)]
        inverse = {}

        def at(k, j):
            return (k, j) if k >= j else (j, k)

        for i in range(8):
            root = lax.rsqrt(swept[i, i])
            reciprocal = root * root
            inverse[i, i] = root
            for j in range(i):
                inverse[i, j] = -swept[i, j] * root
            old = {k: swept[at(k, i)] for k in range(8) if k != i}
            scaled = {k: old[k] * reciprocal for k in old}
            for k in old:
                for j in old:
                    if j <= k:
                        swept[k, j] = swept[k, j] - old[k] * scaled[j]
                swept[at(k, i)] = scaled[k]
            swept[i, i] = -reciprocal
        combined = [total([swept[at(j, i)] * rows[i] for i in range(8)]) for j in range(8)]
        for h in range(g + 1, groups):
            terms = [column(h, first + j) * combined[j] for j in range(8)]
            work[h] = total([jnp.where(inside, 0.0, work[h])] + terms)
        done = None
        for i in range(8):
            row = total([inverse[i, j] * rows[j] for j in range(i + 1)])
            done = row if done is None else jnp.where(sub == i, row, done)
        work[g] = done
    full = jnp.concatenate(work, axis=0)
    row_of = lax.broadcasted_iota(jnp.int32, (size, size), 0)
    column_of = lax.broadcasted_iota(jnp.int32, (size, size), 1)
    return jnp.where(column_of <= row_of, full, 0.0)


def three_parts(values):
    high = values.astype(jnp.bfloat16)
    rest = values - high.astype(jnp.float32)
    middle = rest.astype(jnp.bfloat16)
    low = (rest - middle.astype(jnp.float32)).astype(jnp.bfloat16)
    return high, middle, low


def left_parts(values):
    high, middle, low = three_parts(values)
    return jnp.concatenate([high, high, middle, middle, high, low], axis=1)


def right_parts(values):
    high, middle, low = three_parts(values)
    return jnp.concatenate([high, middle, high, middle, low, high], axis=0)


def unpack(packed_ref, out_ref):
    size = out_ref.shape[0]
    band = packed_ref.shape[1] - size
    count = size // band
    out_ref[...] = jnp.zeros(out_ref.shape, jnp.float32)
    for b in range(count // 2):
        c = count - 1 - b
        out_ref[b * band : (b + 1) * band, b * band :] = packed_ref[b * band : (b + 1) * band, : size - b * band]
        out_ref[c * band : (c + 1) * band, c * band :] = packed_ref[b * band : (b + 1) * band, size - b * band :]


def inverse_factor_kernel(first, last, shift_ref, packed_ref, out_ref, parts_ref):
    size = out_ref.shape[0]
    blocks = size // BLOCK
    if first == 0:
        unpack(packed_ref, out_ref)
    else:
        out_ref[...] = packed_ref[...]
    unit = lax.broadcasted_iota(jnp.int32, (BLOCK, BLOCK), 0) == lax.broadcasted_iota(jnp.int32, (BLOCK, BLOCK), 1)

    def dot(left, right):
        return jnp.dot(left, right, preferred_element_type=jnp.float32)

    def step(j, carry):
        here = pl.ds(pl.multiple_of(j * BLOCK, BLOCK), BLOCK)
        inv = invert_block(out_ref[here, here] + jnp.where(unit, shift_ref[0], 0.0))
        parts_ref[...] = right_parts(out_ref[here, :])
        out_ref[here, :] = dot(left_parts(inv), parts_ref[...])
        out_ref[here, here] = inv
        parts_ref[...] = right_parts(out_ref[here, :])

        def rest(i, carry):
            there = pl.ds(pl.multiple_of(i * BLOCK, BLOCK), BLOCK)
            panel = out_ref[here, there].T
            out_ref[there, here] = jnp.zeros((BLOCK, BLOCK), jnp.float32)
            out_ref[there, :] -= dot(left_parts(panel), parts_ref[...])
            return carry

        return lax.fori_loop(j + 1, blocks, rest, carry)

    lax.fori_loop(first, last, step, 0)
    for j in range(blocks - 1 if last == blocks else 0):
        out_ref[j * BLOCK : (j + 1) * BLOCK, (j + 1) * BLOCK :] = jnp.zeros(
            (BLOCK, size - (j + 1) * BLOCK), jnp.float32
        )


def inverse_factor_of(shift, packed, size, first, last):
    return pl.pallas_call(
        functools.partial(inverse_factor_kernel, first, last),
        out_shape=jax.ShapeDtypeStruct((size, size), jnp.float32),
        in_specs=[pl.BlockSpec(memory_space=pltpu.SMEM), pl.BlockSpec(memory_space=pltpu.VMEM)],
        out_specs=pl.BlockSpec(memory_space=pltpu.VMEM),
        scratch_shapes=[pltpu.VMEM((6 * BLOCK, size), jnp.bfloat16)],
        compiler_params=pltpu.CompilerParams(vmem_limit_bytes=40 * 1024 * 1024),
        cost_estimate=pl.CostEstimate(flops=12 * size**2 * (last - first) * BLOCK, bytes_accessed=8 * size**2, transcendentals=size),
        name="inverse_factor",
    )(shift, packed)


def thirds(values):
    high = lax.reduce_precision(values, 8, 7)
    rest = values - high
    middle = lax.reduce_precision(rest, 8, 7)
    low = rest - middle
    return [part.astype(jnp.bfloat16) for part in (high, middle, low)]


def dot_last(a, b):
    return lax.dot_general(a, b, (((a.ndim - 1,), (b.ndim - 1,)), ((), ())), preferred_element_type=jnp.float32)


def pick_rows(chosen, values):
    return sum(
        jnp.dot(chosen, part, preferred_element_type=jnp.float32) for part in reversed(thirds(values))
    )


def onward(axis, offset):
    count = lax.axis_size(axis)
    return [(i, (i + offset) % count) for i in range(count)]


def gather(values, axis):
    count = lax.axis_size(axis)
    here = lax.axis_index(axis)
    whole = jnp.zeros((count,) + values.shape, values.dtype)
    for offset in range(count):
        part = lax.ppermute(values, axis, onward(axis, offset)) if offset else values
        whole = lax.dynamic_update_index_in_dim(whole, part, (here - offset) % count, 0)
    return whole


def scatter_sum(values, axis):
    count = lax.axis_size(axis)
    here = lax.axis_index(axis)
    rows = values.shape[0] // count
    total = lax.dynamic_slice_in_dim(values, here * rows, rows, 0)
    for offset in range(1, count):
        part = lax.dynamic_slice_in_dim(values, (here + offset) % count * rows, rows, 0)
        total = total + lax.ppermute(part, axis, onward(axis, offset))
    return total


def on_device(jacobian, sample_slot, panel_index, shift_value):
    rows, params = jacobian.shape
    sizes = {axis: lax.axis_size(axis) for axis in EVERY}
    own = {axis: lax.axis_index(axis) for axis in EVERY}
    layers, across = sizes["z"], sizes["x"]
    slab = lax.axis_size(SLAB)
    width = across * rows
    group = layers * width
    members = layers * across
    samples = group * sizes["y"] * sizes["core"]
    pivot_group = panel_index[0] // group
    rotation = panel_index[0] % group
    own_group = lax.axis_index(("y", "core"))
    member = lax.axis_index(("z", "x"))

    tiles, pivots = [], []
    slots = sample_slot
    start = 0
    unit = params // slab // sum(SHARES)
    eights = rows // 8
    strips = with_layout_constraint(jacobian.reshape(eights, 8, slab, params // slab), Layout((0, 2, 1, 3)))
    for chunk, share in enumerate(SHARES):
        if tiles:
            here, tiles[-1], slots = lax.optimization_barrier((jnp.int32(start), tiles[-1], slots))
            if chunk == 1:
                for axis in reversed(EVERY):
                    slots = gather(slots, axis)
            piece = lax.dynamic_slice_in_dim(strips, here * unit, share * unit, axis=3)
        else:
            piece = lax.slice_in_dim(strips, 0, share * unit, axis=3)
        start += share
        piece = with_layout_constraint(piece.transpose(2, 0, 1, 3), Layout((0, 1, 2, 3))).reshape(slab, rows, -1)
        tile = lax.all_to_all(piece, SLAB, split_axis=0, concat_axis=0, tiled=True)
        tile = with_layout_constraint(tile, Layout((0, 1, 2))).reshape(slab * rows, -1)
        near = lax.dynamic_slice_in_dim(tile, pivot_group * width, width, 0)
        tiles.append(tile)
        if chunk == PASSED:
            ring = [near, lax.ppermute(near, "z", onward("z", 1))]
            pivots.append(None)
        else:
            pivots.append(lax.all_gather(near, "z", axis=0, tiled=True))

    ring[1], tiles[-1] = lax.optimization_barrier((ring[1], tiles[-1]))
    for _ in range(2, layers):
        ring.append(lax.ppermute(ring[-1], "z", onward("z", 1)))
    passed = jnp.zeros((group, ring[0].shape[1]), ring[0].dtype)
    for r, part in enumerate(ring):
        passed = lax.dynamic_update_slice_in_dim(passed, part, (own["z"] - r) % layers * width, 0)
    pivots[PASSED] = passed
    for chunk in range(PASSED):
        pivots[chunk], _ = lax.optimization_barrier((pivots[chunk], ring[min(max(chunk, 1), layers - 1)]))
    slots = slots.reshape(samples // group, group)
    pivot_slots = lax.dynamic_index_in_dim(slots, pivot_group, 0, keepdims=False)
    index = jnp.arange(group)
    pick = (index[:, None] == ((pivot_slots - rotation) % group)[None, :]).astype(jnp.bfloat16)

    band = group // (2 * layers)
    low, high = own["z"] * band, (2 * layers - 1 - own["z"]) * band
    panel = lower = upper = 0.0
    for chunk, (tile, gathered) in enumerate(zip(tiles, pivots)):
        ordered = jnp.dot(pick, gathered, preferred_element_type=jnp.float32).astype(jnp.bfloat16)
        panel = panel + dot_last(tile, ordered)
        lower = lower + dot_last(lax.dynamic_slice_in_dim(ordered, low, band, 0), ordered)
        upper = upper + dot_last(lax.dynamic_slice_in_dim(ordered, high, band, 0), ordered)
        if chunk + 1 < len(tiles):
            panel, lower, upper = lax.optimization_barrier((panel, lower, upper))

    place = jnp.arange(group + band)[None, :]
    lower = lax.dynamic_slice_in_dim(jnp.pad(lower, ((0, 0), (0, group))), low, group + band, 1)
    upper = jnp.pad(upper, ((0, 0), (band, 0)))
    packed = jnp.where(place < group - low, lower, upper) / samples
    summed = scatter_sum(packed, "core")
    cut = summed.shape[0] // 2
    one = scatter_sum(scatter_sum(summed[:cut], "x"), "y")
    two = scatter_sum(scatter_sum(summed[cut:], "y"), "x")
    layered = gather(jnp.concatenate([one, two]), "z")
    few = one.shape[0]
    one = gather(gather(layered[:, :few], "y"), "x")
    two = gather(gather(layered[:, few:], "x"), "y")
    packed = jnp.concatenate([one.reshape(-1, layers, few, group + band), two.reshape(-1, layers, few, group + band)])
    packed = gather(packed, "core")
    packed = packed.transpose(2, 0, 1, 3, 4).reshape(layers * band, group + band)

    mine = lax.psum_scatter(panel / samples, SLAB, scatter_dimension=0, tiled=True)

    room = 8 * -(-5 * rows // 128)
    owners = (slots // rows).reshape(-1, members, rows)
    earlier = jnp.arange(rows)[:, None] > jnp.arange(rows)[None, :]
    alike = owners[..., :, None] == owners[..., None, :]
    rank = jnp.sum(alike & earlier, axis=-1)
    rounds = jnp.max(rank) // room + 1
    own_slots = lax.dynamic_index_in_dim(slots, own_group, 0, keepdims=False).reshape(members, rows)
    own_owners = lax.dynamic_index_in_dim(owners, own_group, 0, keepdims=False)
    own_rank = lax.dynamic_index_in_dim(rank, own_group, 0, keepdims=False)
    targets = jnp.arange(members)
    out_slots = member * rows + jnp.arange(rows)

    def exchange_rows(number, rows_here):
        seat = number * room + jnp.arange(room)
        goes = (own_owners[member][None, None, :] == targets[:, None, None]) & (
            own_rank[member][None, None, :] == seat[None, :, None]
        )
        sent = pick_rows(goes.reshape(members * room, rows).astype(jnp.bfloat16), rows_here)
        received = lax.all_to_all(sent, ("z", "x"), split_axis=0, concat_axis=0, tiled=True)
        comes = (own_owners == member)[:, None, :] & (own_rank[:, None, :] == seat[None, :, None])
        names = jnp.max(jnp.where(comes, own_slots[:, None, :], -1), axis=2).reshape(members * room)
        return pick_rows((out_slots[:, None] == names[None, :]).astype(jnp.bfloat16), received)

    blocks = group // BLOCK
    first = blocks // 4
    begun = inverse_factor_of(shift_value, packed, group, 0, first)
    mine, begun = lax.optimization_barrier((mine, begun))
    gram = exchange_rows(0, mine)
    inverse_factor = inverse_factor_of(shift_value, begun, group, first, blocks)
    gram = lax.fori_loop(1, rounds, lambda number, total: total + exchange_rows(number, mine), gram)
    on_pivot = (own_group == pivot_group).astype(jnp.float32)
    shifted_eye = ((out_slots - rotation) % group)[:, None] == index[None, :]
    gram = gram + shift_value[0] * on_pivot * shifted_eye.astype(jnp.float32)
    return lax.dot_general(
        gram, inverse_factor, (((1,), (1,)), ((), ())), precision=HIGHEST, preferred_element_type=jnp.float32
    )


def solution(mesh):
    samp, par = mesh.shape["samp"], mesh.shape["par"]
    y = samp // 2
    x = y if par % y == 0 else 1
    fine = Mesh(mesh.devices.reshape(y, 2, par // x, x), EVERY)
    placed = (P(EVERY, None), P(EVERY), P(), P())
    return jax.shard_map(on_device, mesh=fine, in_specs=placed, out_specs=P(EVERY, None), check_vma=False)
```
